256 devices in a mesh: batch: 8 (over y, core), gx: 8 (over z), gy: 4 (over x).
Axes of the slice: x: 4, y: 4, z: 8, core: 2. Of those that a mesh axis runs over, the one named last changes fastest.
Arguments:
- tokens: bfloat16 [512, 2, 18432], P(None, None, ('batch', 'gy')), may hold values from -6 to 6
- w_query: bfloat16 [18432, 12288], P(('batch', 'gy'), 'gx'), may hold values from -0.046875 to 0.046875
- w_keyval: bfloat16 [18432, 512], P(('batch', 'gy'), 'gx'), may hold values from -0.09375 to 0.09375
- w_out: bfloat16 [12288, 18432], P('gx', ('batch', 'gy')), may hold values from -0.19921875 to 0.19921875
- cache_keys: bfloat16 [512, 2048, 256], P(('batch', 'gx', 'gy')), may hold values from -140 to 140
- cache_values: bfloat16 [512, 2048, 256], P(('batch', 'gx', 'gy')), may hold values from -6 to 6
- lengths: int32 [512], P(('batch', 'gx', 'gy')), may hold values from 512 to 2048, as said below
Outputs:
- mixed: bfloat16 [512, 2, 18432], P('gx', None, ('batch', 'gy'))
The draws below stay inside these ranges and needn't reach their ends.
Inputs may be any that keep to these rules, and one draw needn't show every extreme that they name: `lengths`: every draw has a sequence with 2048 valid positions and one with 512.
All inputs are finite; a program needn't handle non-finite values.
Results may differ from the reference program's by a relative error of at most 0.02.
Values may be sent and summed in bfloat16 or wider, within the bound.
A program may use at most 64 MiB of HBM per device.

```python
import jax
import jax.numpy as jnp
from jax import lax

D = 18432
HQ = 48
HD = 256
S = 2048
STEPS = 2
B = 512
N_BATCH = 8
N_GY = 4


def draw_cache_keys(key, part):
    key = jax.random.fold_in(key, 11)
    first_key = jax.random.fold_in(key, 0)
    base = 2.0 * jax.random.normal(first_key, (B, S, HD), jnp.float32)
    return jnp.clip(base, -12.0, 12.0).astype(jnp.bfloat16)


def draw_lengths(key, part):
    key = jax.random.fold_in(key, 23)
    first_key, second_key = jax.random.split(key, 2)
    values = jax.random.randint(first_key, (B,), S // 4, S + 1)
    order = jax.random.permutation(second_key, B)
    values = values.at[order[0]].set(S).at[order[1]].set(S // 4)
    return values.astype(jnp.int32)


def spiked(entries, key, source, target, shards_of, factor):
    owner, partner = [(jnp.arange(entries.shape[axis_at]) // (entries.shape[axis_at] // shards_of)).reshape([-1 if axis == axis_at else 1 for axis in range(entries.ndim)]) for axis_at in (source, target)]
    chosen = jax.random.permutation(key, shards_of)[partner]
    strong = (owner == chosen) | (owner == (partner + shards_of // 2) % shards_of)
    return jnp.where(strong, factor * entries, entries)


def level_of(key, shape, cuts, low, high):
    factor_of, own = 1.0, jax.random.fold_in(key, 6)
    for position, blocks in cuts:
        draws = jnp.exp(jax.random.uniform(jax.random.fold_in(own, position), (blocks,), jnp.float32, low / len(cuts), high / len(cuts)))
        factor_of = factor_of * jnp.repeat(draws, shape[position] // blocks).reshape([-1 if axis == position else 1 for axis in range(len(shape))])
    return factor_of


def normal_values(key, dims, scale, limit, cuts=(), kind=jnp.bfloat16):
    gain = level_of(key, dims, cuts, -0.22, 0.18) if cuts else 1.0
    drawn = jax.random.normal(key, dims, jnp.float32) * scale * gain
    return jnp.minimum(jnp.maximum(drawn, -limit), limit).astype(kind)


def noise_with(key, shape, spread, limit, cuts, heavy, kind=jnp.bfloat16):
    values = spread * jax.random.normal(key, shape, jnp.float32)
    if cuts:
        values = values * level_of(key, shape, cuts, -0.22, 0.18)
    return jnp.clip(spiked(values, jax.random.fold_in(key, 3), *heavy), -limit, limit).astype(kind)


def setup_inputs(seed: int = 0) -> dict:
    seeds = jax.random.split(jax.random.key(seed), 8)
    tokens = noise_with(seeds[0], (B, STEPS, D), 1.0, 6.0, ((2, 32),), (2, 0, 32, 2.75))
    w_query = normal_values(seeds[1], (D, HQ * HD), D ** -0.5, 0.046875, ((0, 32), (1, 8)))
    w_keyval = normal_values(seeds[2], (D, 2 * HD), (D // 4) ** -0.5, 0.09375, ((0, 32), (1, 8)))
    w_out = normal_values(seeds[3], (HQ * HD, D), 0.03, 0.19921875, ((0, 8), (1, 32)))
    cache_keys = draw_cache_keys(jax.random.fold_in(seeds[7], 71), 0)
    cache_values = normal_values(seeds[5], (B, S, HD), 1.0, 6.0, ((0, 256),))
    lengths = draw_lengths(jax.random.fold_in(seeds[7], 71), 0)
    return dict(tokens=tokens, w_query=w_query, w_keyval=w_keyval, w_out=w_out, cache_keys=cache_keys, cache_values=cache_values, lengths=lengths)


def rotate(values, positions):
    half_width = values.shape[-1] // 2
    freqs = 10000.0 ** (-(jnp.arange(half_width, dtype=jnp.float32) * 2.0 / values.shape[-1]))
    angles = positions[..., None] * freqs
    cosine = jnp.cos(angles)
    sine = jnp.sin(angles)
    first_half = values[..., :half_width]
    second_half = values[..., half_width:]
    return jnp.concatenate([first_half * cosine - second_half * sine, second_half * cosine + first_half * sine], axis=-1)


def attend(queries, keys_cache, values_cache, new_keys, new_values, length_now):
    scaling = 1.0 / (queries.shape[-1] ** 0.5)
    cached = jnp.einsum('thd,sd->ths', queries.astype(jnp.float32), keys_cache.astype(jnp.float32)) * scaling
    valid = jnp.arange(keys_cache.shape[0], dtype=jnp.int32) < length_now
    cached = jnp.where(valid[None, None, :], cached, -1e30)
    fresh = jnp.einsum('thd,ud->thu', queries.astype(jnp.float32), new_keys.astype(jnp.float32)) * scaling
    steps_here = queries.shape[0]
    causal = jnp.arange(steps_here)[None, :] <= jnp.arange(steps_here)[:, None]
    fresh = jnp.where(causal[:, None, :], fresh, -1e30)
    highest = jnp.maximum(cached.max(-1, keepdims=True), fresh.max(-1, keepdims=True))
    exp_cached = jnp.exp(cached - highest)
    exp_fresh = jnp.exp(fresh - highest)
    denom = exp_cached.sum(-1, keepdims=True) + exp_fresh.sum(-1, keepdims=True)
    probs_cached = (exp_cached / denom).astype(jnp.bfloat16)
    probs_fresh = (exp_fresh / denom).astype(jnp.bfloat16)
    result = jnp.einsum('ths,sd->thd', probs_cached.astype(jnp.float32), values_cache.astype(jnp.float32))
    result = result + jnp.einsum('thu,ud->thd', probs_fresh.astype(jnp.float32), new_values.astype(jnp.float32))
    return result.reshape(steps_here, -1).astype(jnp.bfloat16)


def reference(tokens, w_query, w_keyval, w_out, cache_keys, cache_values, lengths):
    joined = jnp.concatenate([w_query, w_keyval], axis=1)
    flat = tokens.reshape(B * STEPS, D)
    block_total = N_BATCH * N_GY
    block_width = D // block_total

    def accumulate(carry, index):
        rows_in = lax.dynamic_slice_in_dim(flat, index * block_width, block_width, 1)
        weights_in = lax.dynamic_slice_in_dim(joined, index * block_width, block_width, 0)
        return carry + jnp.dot(rows_in, weights_in, preferred_element_type=jnp.float32), None

    summed, unused = lax.scan(accumulate, jnp.zeros((B * STEPS, joined.shape[1]), jnp.float32),
                              jnp.arange(block_total, dtype=jnp.int32))
    projected = summed.astype(jnp.bfloat16)
    queries = projected[:, :HQ * HD].reshape(B, STEPS, HQ, HD)
    new_keys = projected[:, HQ * HD:HQ * HD + HD].reshape(B, STEPS, HD)
    new_values = projected[:, HQ * HD + HD:].reshape(B, STEPS, HD)
    positions = (lengths[:, None] + jnp.arange(STEPS, dtype=jnp.int32)[None, :]).astype(jnp.float32)
    rot_queries = rotate(queries.astype(jnp.float32), positions[:, :, None]).astype(jnp.bfloat16)
    rot_keys = rotate(new_keys.astype(jnp.float32), positions).astype(jnp.bfloat16)
    attended = lax.map(lambda items: attend(*items),
                       (rot_queries, cache_keys, cache_values, rot_keys, new_values, lengths))
    mixed = jnp.dot(attended.reshape(B * STEPS, HQ * HD), w_out, preferred_element_type=jnp.float32)
    return mixed.astype(jnp.bfloat16).reshape(B, STEPS, D)
```

```python
import functools

import jax
import jax.numpy as jnp
import numpy as np
from jax import lax
from jax.experimental import pallas as pl
from jax.experimental.pallas import tpu as pltpu
from jax.sharding import PartitionSpec as P

MESH = pl.DeviceIdType.MESH
BF = jnp.bfloat16
F32 = jnp.float32
NX, NY, NZ = 4, 4, 8
D_LOC, COLS = 576, 1536
HD, SLOTS = 256, 2048
LEFT, RIGHT = 768, 896


def dot_nt(a, b):
    return lax.dot_general(a, b, (((1,), (1,)), ((), ())), preferred_element_type=F32)


def dot_nn(a, b):
    return lax.dot_general(a, b, (((1,), (0,)), ((), ())), preferred_element_type=F32)


def grid_of(rows, cols):
    return (
        lax.broadcasted_iota(jnp.int32, (rows, cols), 0),
        lax.broadcasted_iota(jnp.int32, (rows, cols), 1),
    )


def one_hot(hit):
    return jnp.where(hit, 1.0, 0.0).astype(BF)


def kernel(
    tok, wq, wkv, wo, ck, cv, lens, freq, out,
    vtok, vwq, vwkv, vwo, vk, vv, vfreq, xp,
    sib_s, sib_r, part0, part1, part2, part3, got0, got1, got2, got3,
    mid0, mid1, mid2, mid3, fin0, fin1, fin2, fin3,
    stack, qs, qr, ats, atr, g, zpart, zs, zr,
    ld_sem, send_sem, recv_sem,
):
    b = lax.axis_index("batch")
    z = lax.axis_index("gx")
    x = lax.axis_index("gy")
    y, c = b // 2, b % 2

    loads = {}
    for k, (name, src, dst) in enumerate([
        ("tok", tok, vtok),
        ("wq", wq, vwq),
        ("wkv", wkv, vwkv.at[pl.ds(0, 64)]),
        ("freq", freq, vfreq),
        ("k", ck, vk),
        ("v", cv, vv),
        ("wo", wo, vwo.at[pl.ds(0, D_LOC)]),
        ("wo2", wo.at[pl.ds(512, 64)], vwo.at[pl.ds(D_LOC, 64)]),
    ]):
        loads[name] = pltpu.make_async_copy(src, dst, ld_sem.at[k])
        loads[name].start()

    def at_x(o):
        return (b, z, (x + o) % NX)

    def at_y(o):
        return ((b + 2 * o) % (2 * NY), z, x)

    def at_z(o):
        return (b, (z + o) % NZ, x)

    sibling = (y * 2 + (1 - c), z, x)

    barrier = pltpu.get_barrier_semaphore()
    partners = [sibling] + [at_x(o) for o in (1, 2, 3)] + [at_y(o) for o in (1, 2, 3)]
    partners += [at_z(o) for o in range(1, NZ)]
    for partner in partners:
        pl.semaphore_signal(barrier, inc=1, device_id=partner, device_id_type=MESH)

    count = [0]
    sent = []

    def copy_to(src, dst, device):
        k = count[0]
        count[0] += 1
        copy = pltpu.make_async_remote_copy(
            src_ref=src, dst_ref=dst, send_sem=send_sem.at[k], recv_sem=recv_sem.at[k],
            device_id=device, device_id_type=MESH,
        )
        copy.start()
        sent.append(copy)
        return copy

    vwkv[64:128, :] = jnp.zeros((64, D_LOC), BF)
    r, k = grid_of(256, 256)
    perm = one_hot(
        k == (r & 1) * 128 + ((r >> 6) & 1) * 64 + ((r >> 1) & 7) * 8 + ((r >> 4) & 3) * 2 + (r >> 7)
    )
    loads["tok"].wait()
    for yy in range(NY):
        both = jnp.concatenate(
            [vtok[0, :, yy * 128:(yy + 1) * 128], vtok[1, :, yy * 128:(yy + 1) * 128]], axis=1
        )
        rows = dot_nt(perm, both).astype(BF)
        for s in range(2):
            for cc in range(2):
                at = (s * 2 + cc) * 64
                xp[s, cc, yy * 64:(yy + 1) * 64, :] = rows[at:at + 64]
    pl.semaphore_wait(barrier, len(partners))
    loads["wq"].wait()
    loads["wkv"].wait()

    parts, gots = (part0, part1, part2, part3), (got0, got1, got2, got3)
    mids, fins = (mid0, mid1, mid2, mid3), (fin0, fin1, fin2, fin3)
    first_x = (True, False, False, True)

    def project(s, side, core):
        rows = xp[s, core]
        if side == 0:
            return dot_nn(rows, vwq[:, 0:LEFT])
        return jnp.concatenate([dot_nn(rows, vwq[:, LEFT:COLS]), dot_nt(rows, vwkv[...])], axis=1)

    def width(side):
        return LEFT if side == 0 else RIGHT

    def cols_of(side):
        return pl.ds(0, LEFT) if side == 0 else pl.ds(LEFT, RIGHT)

    stage1 = {}

    def start_unit(u):
        s, side = divmod(u, 2)
        cols = cols_of(side)
        sib_s[s, :, cols] = project(s, side, 1 - c).astype(BF)
        swap = copy_to(sib_s.at[s, :, cols], sib_r.at[s, :, cols], sibling)
        own = project(s, side, c)
        swap.wait_recv()
        total = (own + sib_r[s, :, cols].astype(F32)).astype(BF)
        for yy in range(NY):
            for xx in range(NX):
                at = (yy * NX + xx) * 16
                lead = (xx, yy) if first_x[u] else (yy, xx)
                parts[u][lead[0], lead[1]] = total[at:at + 16]
        me, to = (x, at_x) if first_x[u] else (y, at_y)
        stage1[u] = [
            copy_to(parts[u].at[(me + o) % 4], gots[u].at[o - 1], to(o)) for o in (2, 1, 3)
        ]

    stage2 = {}

    def middle_unit(u):
        me, to, other = (x, at_y, y) if first_x[u] else (y, at_x, x)
        for copy in stage1[u]:
            copy.wait_recv()
        total = parts[u][me].astype(F32)
        for o in range(3):
            total = total + gots[u][o].astype(F32)
        mids[u][...] = total.astype(BF)
        stage2[u] = [copy_to(mids[u].at[(other + o) % 4], fins[u].at[o - 1], to(o)) for o in (2, 1, 3)]

    def finish_unit(u):
        other = y if first_x[u] else x
        for copy in stage2[u]:
            copy.wait_recv()
        total = mids[u][other].astype(F32)
        for o in range(3):
            total = total + fins[u][o].astype(F32)
        return total.astype(BF)

    r, k = grid_of(128, 128)
    slot = r & 15
    to_groups = one_hot((slot < 14) & (k == (slot >> 1) * 16 + (r >> 4) * 2 + (slot & 1)))
    r, k = grid_of(128, 256)
    place = one_hot((r < 64) & (k == r + (z % 4) * 64))

    exchange = {}

    def send_queries(s):
        left = finish_unit(2 * s)
        right = finish_unit(2 * s + 1)
        for h in range(3):
            stack[s, h * 16:(h + 1) * 16] = left[:, h * HD:(h + 1) * HD]
            stack[s, (h + 3) * 16:(h + 4) * 16] = right[:, h * HD:(h + 1) * HD]
        stack[s, 96:112] = dot_nn(right[:, LEFT:RIGHT], place).astype(BF)
        stack[s, 112:128] = jnp.zeros((16, HD), BF)
        grouped = dot_nn(to_groups, stack[s]).astype(BF)
        for zz in range(NZ):
            qs[s, zz] = grouped[zz * 16:(zz + 1) * 16]
        exchange[s] = [
            copy_to(qs.at[s, (z + o) % NZ], qr.at[s, z], at_z(o)) for o in (4, 3, 5, 2, 6, 1, 7)
        ]
        qr[s, z] = qs[s, z]

    loads["freq"].wait()
    r, _ = grid_of(8, 128)
    length = jnp.where((r & 2) == 0, lens[0], lens[1])
    angle = (length + (r & 1)).astype(F32) * vfreq[...]
    cosine, sine = jnp.cos(angle), jnp.sin(angle)

    r, k = grid_of(128, 128)
    pick_key = one_hot((r < 2) & ((k & 15) == 12 + r) & ((k >> 4) < 4))
    pick_value = one_hot((r < 2) & ((k & 15) == 12 + r) & ((k >> 4) >= 4))
    odd = (r & 1) == 1
    causal = k <= (r & 1)

    def attention(s):
        for copy in exchange[s]:
            copy.wait_recv()
        raw = qr[s].reshape(128, HD)
        cos_rows = jnp.where(odd, cosine[2 * s + 1:2 * s + 2], cosine[2 * s:2 * s + 1])
        sin_rows = jnp.where(odd, sine[2 * s + 1:2 * s + 2], sine[2 * s:2 * s + 1])

        def rotate(values):
            u, w = values[:, :128], values[:, 128:]
            return jnp.concatenate(
                [u * cos_rows - w * sin_rows, w * cos_rows + u * sin_rows], axis=1
            ).astype(BF)

        queries = rotate(raw.astype(F32))
        new_keys = rotate(dot_nn(pick_key, raw))
        new_values = dot_nn(pick_value, raw).astype(BF)
        if s == 0:
            loads["k"].wait()
        scale = 1.0 / HD**0.5
        cached = dot_nt(queries, vk[s]) * scale
        _, column = grid_of(128, SLOTS)
        cached = jnp.where(column < lens[s], cached, -1e30)
        fresh = jnp.where(causal, dot_nt(queries, new_keys) * scale, -1e30)
        highest = jnp.maximum(cached.max(-1, keepdims=True), fresh.max(-1, keepdims=True))
        cached = jnp.exp(cached - highest)
        fresh = jnp.exp(fresh - highest)
        denom = cached.sum(-1, keepdims=True) + fresh.sum(-1, keepdims=True)
        if s == 0:
            loads["v"].wait()
        result = dot_nn(cached.astype(BF), vv[s]) + dot_nn(fresh.astype(BF), new_values)
        result = (result / denom).astype(BF)
        for zz in range(NZ):
            ats[s, zz] = result[zz * 16:(zz + 1) * 16]
        exchange[s] = [
            copy_to(ats.at[s, (z + o) % NZ], atr.at[s, z], at_z(o)) for o in (4, 3, 5, 2, 6, 1, 7)
        ]
        atr[s, z] = ats[s, z]

    halves = (pl.ds(0, COLS // 2), pl.ds(COLS // 2, COLS // 2))
    to_heads = one_hot((r < 96) & (k == ((r >> 1) & 7) * 16 + (r >> 4) * 2 + (r & 1)))
    gather1, gather2, siblings = {}, {}, {0: [], 1: []}

    def gather_start(s):
        for copy in exchange[s]:
            copy.wait_recv()
        heads = dot_nn(to_heads, atr[s].reshape(128, HD)).astype(BF)
        for h in range(6):
            g[s, y, c, x, :, h * HD:(h + 1) * HD] = heads[h * 16:(h + 1) * 16]
        mine_l = g.at[s, y, c, x, :, halves[0]]
        mine_r = g.at[s, y, c, x, :, halves[1]]
        gather1[s] = []
        for o in (2, 1, 3):
            gather1[s].append(copy_to(mine_l, mine_l, at_x(o)))
            gather1[s].append(copy_to(mine_r, mine_r, at_y(o)))
        siblings[s].append(copy_to(g.at[s, y, c, x], g.at[s, y, c, x], sibling))

    def gather_middle(s):
        for copy in gather1[s]:
            copy.wait_recv()
        block_l = g.at[s, y, c, :, :, halves[0]]
        block_r = g.at[s, :, c, x, :, halves[1]]
        gather2[s] = []
        for o in (2, 1, 3):
            gather2[s].append((copy_to(block_l, block_l, at_y(o)), copy_to(block_r, block_r, at_x(o)), o))
        for o in (1, 2, 3):
            piece = g.at[s, y, c, (x + o) % NX, :, halves[0]]
            siblings[s].append(copy_to(piece, piece, sibling))
            piece = g.at[s, (y + o) % NY, c, x, :, halves[1]]
            siblings[s].append(copy_to(piece, piece, sibling))

    def gather_end(s):
        for from_y, from_x, o in gather2[s]:
            from_y.wait_recv()
            block = g.at[s, (y + 4 - o) % NY, c, :, :, halves[0]]
            siblings[s].append(copy_to(block, block, sibling))
            from_x.wait_recv()
            block = g.at[s, :, c, (x + 4 - o) % NX, :, halves[1]]
            siblings[s].append(copy_to(block, block, sibling))
        for copy in siblings[s]:
            copy.wait_recv()

    low = lax.broadcasted_iota(jnp.int32, (32, 128), 1) < 64

    def output_terms(s):
        if s == 0:
            loads["wo"].wait()
            loads["wo2"].wait()
        terms = dot_nt(g[s].reshape(512, COLS), vwo[...])
        for bb in range(8):
            mine = terms[bb * 64:(bb + 1) * 64]
            for cb in range(4):
                for half in range(2):
                    zpart[s, bb, 2 * cb + half] = mine[half * 32:(half + 1) * 32, cb * 128:(cb + 1) * 128]
            zpart[s, bb, 8] = jnp.where(low, mine[:32, 512:640], mine[32:, 512:640])

    ring = {}

    def ring_step(s, step):
        if step == 0:
            far = zpart[s, (z + 4) % NZ].astype(BF)
            zs[s, 0, 0, 0:5] = far[0:5]
            zs[s, 1, 0, 0:4] = far[5:9]
            ring[s] = [
                copy_to(zs.at[s, 0, 0, pl.ds(0, 5)], zr.at[s, 0, 0, pl.ds(0, 5)], at_z(1)),
                copy_to(zs.at[s, 1, 0, pl.ds(0, 4)], zr.at[s, 1, 0, pl.ds(0, 4)], at_z(7)),
            ]
            return
        copies = []
        for way in range(2):
            ring[s][way].wait_recv()
            dest = (z + 4 - step) % NZ if way == 0 else (z + 4 + step) % NZ
            own = zpart[s, dest]
            if step == 1:
                if way == 0:
                    zs[s, 0, 1, 0:5] = (own[0:5] + zr[s, 0, 0, 0:5].astype(F32)).astype(BF)
                    zs[s, 0, 1, 5:9] = own[5:9].astype(BF)
                else:
                    zs[s, 1, 1, 0:5] = own[0:5].astype(BF)
                    zs[s, 1, 1, 5:9] = (own[5:9] + zr[s, 1, 0, 0:4].astype(F32)).astype(BF)
            else:
                zs[s, way, step] = (own + zr[s, way, step - 1].astype(F32)).astype(BF)
            copies.append(copy_to(zs.at[s, way, step], zr.at[s, way, step], at_z(1 if way == 0 else 7)))
        ring[s] = copies

    def ring_end(s):
        for copy in ring[s]:
            copy.wait_recv()
        total = zpart[s, z] + zr[s, 0, 3].astype(F32) + zr[s, 1, 3].astype(F32)
        return total.astype(BF)

    for u in range(4):
        start_unit(u)
    for u in (0, 1):
        middle_unit(u)
    send_queries(0)
    for u in (2, 3):
        middle_unit(u)
    attention(0)
    send_queries(1)
    gather_start(0)
    attention(1)
    gather_middle(0)
    gather_start(1)
    gather_end(0)
    output_terms(0)
    ring_step(0, 0)
    gather_middle(1)
    ring_step(0, 1)
    gather_end(1)
    output_terms(1)
    ring_step(1, 0)
    ring_step(0, 2)
    ring_step(1, 1)
    ring_step(0, 3)
    ring_step(1, 2)
    first = ring_end(0)
    ring_step(1, 3)
    second = ring_end(1)

    from_row = (k == ((r >> 1) & 1) * 64 + ((r >> 2) & 3) * 16 + (r >> 4) * 2 + (r & 1))
    to_rows = one_hot(from_row)
    for cb in range(4):
        both = jnp.concatenate(
            [first[2 * cb:2 * cb + 2].reshape(64, 128), second[2 * cb:2 * cb + 2].reshape(64, 128)], axis=0
        )
        out[:, cb * 128:(cb + 1) * 128] = dot_nn(to_rows, both).astype(BF)
    tails = jnp.concatenate([first[8], first[8], second[8], second[8]], axis=0)
    in_low = one_hot(from_row & ((k & 32) == 0))
    in_high = one_hot(from_row & ((k & 32) != 0))
    tail = dot_nn(in_low, tails) + pltpu.roll(dot_nn(in_high, tails), 64, 1)
    out[:, 512:576] = tail[:, :64].astype(BF)

    for copy in sent:
        copy.wait_send()


def local(tokens, w_query, w_keyval, w_out, cache_keys, cache_values, lengths):
    freqs = 10000.0 ** (-(np.arange(128, dtype=np.float32) * np.float32(2.0) / np.float32(256)))
    freqs = jnp.asarray(np.broadcast_to(freqs.astype(np.float32)[None], (8, 128)))
    vm = pltpu.VMEM
    units = (LEFT, RIGHT, LEFT, RIGHT)
    scratch = [
        vm((2, D_LOC, 512), BF), vm((D_LOC, COLS), BF), vm((128, D_LOC), BF), vm((640, COLS), BF),
        vm((2, SLOTS, HD), BF), vm((2, SLOTS, HD), BF), vm((8, 128), F32), vm((2, 2, 256, D_LOC), BF),
        vm((2, 256, LEFT + RIGHT), BF), vm((2, 256, LEFT + RIGHT), BF),
        *[vm((4, 4, 16, w), BF) for w in units],
        *[vm((3, 4, 16, w), BF) for w in units],
        *[vm((4, 16, w), BF) for w in units],
        *[vm((3, 16, w), BF) for w in units],
        vm((2, 128, HD), BF),
        *[vm((2, NZ, 16, HD), BF) for _ in range(4)],
        vm((2, NY, 2, NX, 16, COLS), BF),
        vm((2, NZ, 9, 32, 128), F32),
        vm((2, 2, 4, 9, 32, 128), BF), vm((2, 2, 4, 9, 32, 128), BF),
        pltpu.SemaphoreType.DMA((8,)), pltpu.SemaphoreType.DMA((160,)), pltpu.SemaphoreType.DMA((160,)),
    ]
    hbm = pl.BlockSpec(memory_space=pl.ANY)
    result = pl.pallas_call(
        kernel,
        out_shape=jax.ShapeDtypeStruct((128, D_LOC), BF),
        in_specs=[hbm] * 6 + [pl.BlockSpec(memory_space=pltpu.SMEM), hbm],
        out_specs=pl.BlockSpec(memory_space=pltpu.VMEM),
        scratch_shapes=scratch,
        compiler_params=pltpu.CompilerParams(
            collective_id=0, has_side_effects=True, vmem_limit_bytes=56 * 2**20
        ),
        cost_estimate=pl.CostEstimate(flops=4 * 10**9, bytes_accessed=10**7, transcendentals=10**6),
        name="layer",
    )(
        tokens.transpose(1, 2, 0), w_query, w_keyval.T, w_out.T, cache_keys, cache_values, lengths, freqs
    )
    return result.reshape(64, 2, D_LOC)


def solution(mesh):
    placed = (
        P(None, None, ("batch", "gy")),
        P(("batch", "gy"), "gx"),
        P(("batch", "gy"), "gx"),
        P("gx", ("batch", "gy")),
        P(("batch", "gx", "gy"), None, None),
        P(("batch", "gx", "gy"), None, None),
        P(("batch", "gx", "gy")),
    )
    return jax.shard_map(
        local, mesh=mesh, in_specs=placed, out_specs=P("gx", None, ("batch", "gy")), check_vma=False
    )
```

```python
import functools

import jax
import jax.numpy as jnp
import numpy as np
from jax import lax
from jax.experimental import pallas as pl
from jax.experimental.pallas import tpu as pltpu
from jax.sharding import PartitionSpec as P

MESH = pl.DeviceIdType.MESH
BF = jnp.bfloat16
F32 = jnp.float32
NX, NY, NZ = 4, 4, 8
D_LOC, COLS = 576, 1536
HD, SLOTS = 256, 2048
SEND_SLOTS = 32
SWAP, STAGE1, STAGE2, QUERIES, RESULTS, GATHER1, FORWARD, GATHER2, RING = 0, 4, 8, 12, 14, 16, 18, 20, 32
LEFT, RIGHT = 768, 896


def dot_nt(a, b):
    return lax.dot_general(a, b, (((1,), (1,)), ((), ())), preferred_element_type=F32)


def dot_nn(a, b):
    return lax.dot_general(a, b, (((1,), (0,)), ((), ())), preferred_element_type=F32)


def grid_of(rows, cols):
    return (
        lax.broadcasted_iota(jnp.int32, (rows, cols), 0),
        lax.broadcasted_iota(jnp.int32, (rows, cols), 1),
    )


def one_hot(hit):
    return jnp.where(hit, 1.0, 0.0).astype(BF)


def kernel(
    tok, wq, wkv, wo, ck, cv, lens_in, out,
    vtok, vwq, vwkv, vwo, vk, vv, lens, xp,
    sib_s, sib_r, part0, part1, part2, part3, got0, got1, got2, got3,
    mid0, mid1, mid2, mid3, fin0, fin1, fin2, fin3,
    stack, qs, qr, ats, atr, g, zpart, zs, zr,
    ld_sem, send_sem, recv_sem,
):
    b = lax.axis_index("batch")
    z = lax.axis_index("gx")
    x = lax.axis_index("gy")
    y, c = b // 2, b % 2

    loads = {}
    for k, (name, src, dst) in enumerate([
        ("tok", tok, vtok),
        ("wq", wq, vwq),
        ("wkv", wkv, vwkv.at[pl.ds(0, 64)]),
        ("lens", lens_in, lens),
        ("k", ck, vk),
        ("v", cv, vv),
        ("wo", wo, vwo.at[pl.ds(0, D_LOC)]),
        ("wo2", wo.at[pl.ds(512, 64)], vwo.at[pl.ds(D_LOC, 64)]),
    ]):
        loads[name] = pltpu.make_async_copy(src, dst, ld_sem.at[k])
        loads[name].start()

    def at_x(o):
        return (b, z, (x + o) % NX)

    def at_y(o):
        return ((b + 2 * o) % (2 * NY), z, x)

    def at_z(o):
        return (b, (z + o) % NZ, x)

    sibling = (y * 2 + (1 - c), z, x)

    barrier = pltpu.get_barrier_semaphore()
    partners = [sibling] + [at_x(o) for o in (1, 2, 3)] + [at_y(o) for o in (1, 2, 3)]
    partners += [at_z(o) for o in range(1, NZ)]
    for partner in partners:
        pl.semaphore_signal(barrier, inc=1, device_id=partner, device_id_type=MESH)

    slots = [None] * SEND_SLOTS
    count = [0]

    def copy_to(src, dst, device, sem):
        k = count[0] % SEND_SLOTS
        count[0] += 1
        if slots[k] is not None:
            slots[k].wait_send()
        copy = pltpu.make_async_remote_copy(
            src_ref=src, dst_ref=dst, send_sem=send_sem.at[k], recv_sem=recv_sem.at[sem],
            device_id=device, device_id_type=MESH,
        )
        copy.start()
        slots[k] = copy

    def arrived(ref, sem):
        pltpu.make_async_copy(ref, ref, recv_sem.at[sem]).wait()

    vwkv[64:128, :] = jnp.zeros((64, D_LOC), BF)
    r, k = grid_of(256, 256)
    perm = one_hot(
        k == (r & 1) * 128 + ((r >> 6) & 1) * 64 + ((r >> 1) & 7) * 8 + ((r >> 4) & 3) * 2 + (r >> 7)
    )
    loads["tok"].wait()
    for yy in range(NY):
        both = jnp.concatenate(
            [vtok[0, :, yy * 128:(yy + 1) * 128], vtok[1, :, yy * 128:(yy + 1) * 128]], axis=1
        )
        rows = dot_nt(perm, both).astype(BF)
        for s in range(2):
            for cc in range(2):
                at = (s * 2 + cc) * 64
                xp[s, cc, yy * 64:(yy + 1) * 64, :] = rows[at:at + 64]
    loads["wq"].wait()
    loads["wkv"].wait()

    parts, gots = (part0, part1, part2, part3), (got0, got1, got2, got3)
    mids, fins = (mid0, mid1, mid2, mid3), (fin0, fin1, fin2, fin3)
    first_x = (True, False, False, True)

    def project(s, side, core):
        rows = xp[s, core]
        if side == 0:
            return dot_nn(rows, vwq[:, 0:LEFT])
        return jnp.concatenate([dot_nn(rows, vwq[:, LEFT:COLS]), dot_nt(rows, vwkv[...])], axis=1)

    def width(side):
        return LEFT if side == 0 else RIGHT

    def cols_of(side):
        return pl.ds(0, LEFT) if side == 0 else pl.ds(LEFT, RIGHT)

    def swap_unit(u):
        s, side = divmod(u, 2)
        cols = cols_of(side)
        sib_s[s, :, cols] = project(s, side, 1 - c).astype(BF)
        if u == 0:
            pl.semaphore_wait(barrier, len(partners))
        copy_to(sib_s.at[s, :, cols], sib_r.at[s, :, cols], sibling, SWAP + u)

    def start_unit(u):
        s, side = divmod(u, 2)
        cols = cols_of(side)
        own = project(s, side, c)
        arrived(sib_r.at[s, :, cols], SWAP + u)
        total = (own + sib_r[s, :, cols].astype(F32)).astype(BF)
        for yy in range(NY):
            for xx in range(NX):
                at = (yy * NX + xx) * 16
                lead = (xx, yy) if first_x[u] else (yy, xx)
                parts[u][lead[0], lead[1]] = total[at:at + 16]
        me, to = (x, at_x) if first_x[u] else (y, at_y)
        for o in (2, 1, 3):
            copy_to(parts[u].at[(me + o) % 4], gots[u].at[o - 1], to(o), STAGE1 + u)

    def middle_unit(u):
        me, to, other = (x, at_y, y) if first_x[u] else (y, at_x, x)
        arrived(gots[u], STAGE1 + u)
        total = parts[u][me].astype(F32)
        for o in range(3):
            total = total + gots[u][o].astype(F32)
        mids[u][...] = total.astype(BF)
        for o in (2, 1, 3):
            copy_to(mids[u].at[(other + o) % 4], fins[u].at[o - 1], to(o), STAGE2 + u)

    def finish_unit(u):
        other = y if first_x[u] else x
        arrived(fins[u], STAGE2 + u)
        total = mids[u][other].astype(F32)
        for o in range(3):
            total = total + fins[u][o].astype(F32)
        return total.astype(BF)

    r, k = grid_of(128, 128)
    slot = r & 15
    to_groups = one_hot((slot < 14) & (k == (slot >> 1) * 16 + (r >> 4) * 2 + (slot & 1)))
    r, k = grid_of(128, 256)
    place = one_hot((r < 64) & (k == r + (z % 4) * 64))

    def send_queries(s):
        left = finish_unit(2 * s)
        right = finish_unit(2 * s + 1)
        for h in range(3):
            stack[s, h * 16:(h + 1) * 16] = left[:, h * HD:(h + 1) * HD]
            stack[s, (h + 3) * 16:(h + 4) * 16] = right[:, h * HD:(h + 1) * HD]
        stack[s, 96:112] = dot_nn(right[:, LEFT:RIGHT], place).astype(BF)
        stack[s, 112:128] = jnp.zeros((16, HD), BF)
        grouped = dot_nn(to_groups, stack[s]).astype(BF)
        for zz in range(NZ):
            qs[s, zz] = grouped[zz * 16:(zz + 1) * 16]
        for o in (4, 3, 5, 2, 6, 1, 7):
            copy_to(qs.at[s, (z + o) % NZ], qr.at[s, z], at_z(o), QUERIES + s)
        qr[s, z] = qs[s, z]

    loads["lens"].wait()
    r, k = grid_of(8, 128)
    freqs = jnp.exp(k.astype(F32) * (-np.log(10000.0) / 128))
    length = jnp.where((r & 2) == 0, lens[0], lens[1])
    angle = (length + (r & 1)).astype(F32) * freqs
    cosine, sine = jnp.cos(angle), jnp.sin(angle)

    r, k = grid_of(128, 128)
    pick_key = one_hot((r < 2) & ((k & 15) == 12 + r) & ((k >> 4) < 4))
    pick_value = one_hot((r < 2) & ((k & 15) == 12 + r) & ((k >> 4) >= 4))
    odd = (r & 1) == 1
    causal = k <= (r & 1)

    def attention(s):
        arrived(qr.at[s, pl.ds(0, NZ - 1)], QUERIES + s)
        raw = qr[s].reshape(128, HD)
        cos_rows = jnp.where(odd, cosine[2 * s + 1:2 * s + 2], cosine[2 * s:2 * s + 1])
        sin_rows = jnp.where(odd, sine[2 * s + 1:2 * s + 2], sine[2 * s:2 * s + 1])

        def rotate(values):
            u, w = values[:, :128], values[:, 128:]
            return jnp.concatenate(
                [u * cos_rows - w * sin_rows, w * cos_rows + u * sin_rows], axis=1
            ).astype(BF)

        queries = rotate(raw.astype(F32))
        new_keys = rotate(dot_nn(pick_key, raw))
        new_values = dot_nn(pick_value, raw).astype(BF)
        if s == 0:
            loads["k"].wait()
        scale = 1.0 / HD**0.5
        cached = dot_nt(queries, vk[s]) * scale
        _, column = grid_of(128, SLOTS)
        cached = jnp.where(column < lens[s], cached, -1e30)
        fresh = jnp.where(causal, dot_nt(queries, new_keys) * scale, -1e30)
        highest = jnp.maximum(cached.max(-1, keepdims=True), fresh.max(-1, keepdims=True))
        cached = jnp.exp(cached - highest)
        fresh = jnp.exp(fresh - highest)
        denom = cached.sum(-1, keepdims=True) + fresh.sum(-1, keepdims=True)
        if s == 0:
            loads["v"].wait()
        result = dot_nn(cached.astype(BF), vv[s]) + dot_nn(fresh.astype(BF), new_values)
        result = (result / denom).astype(BF)
        for zz in range(NZ):
            ats[s, zz] = result[zz * 16:(zz + 1) * 16]
        for o in (4, 3, 5, 2, 6, 1, 7):
            copy_to(ats.at[s, (z + o) % NZ], atr.at[s, z], at_z(o), RESULTS + s)
        atr[s, z] = ats[s, z]

    halves = (pl.ds(0, COLS // 2), pl.ds(COLS // 2, COLS // 2))
    to_heads = one_hot((r < 96) & (k == ((r >> 1) & 7) * 16 + (r >> 4) * 2 + (r & 1)))

    def gather_start(s):
        arrived(atr.at[s, pl.ds(0, NZ - 1)], RESULTS + s)
        heads = dot_nn(to_heads, atr[s].reshape(128, HD)).astype(BF)
        for h in range(6):
            g[s, y, c, x, :, h * HD:(h + 1) * HD] = heads[h * 16:(h + 1) * 16]
        mine_l = g.at[s, y, c, x, :, halves[0]]
        mine_r = g.at[s, y, c, x, :, halves[1]]
        for o in (2, 1, 3):
            copy_to(mine_l, mine_l, at_x(o), GATHER1 + s)
            copy_to(mine_r, mine_r, at_y(o), GATHER1 + s)
        copy_to(g.at[s, y, c, x], g.at[s, y, c, x], sibling, FORWARD + s)

    def gather_middle(s):
        arrived(g.at[s, 0, 0, pl.ds(0, 3)], GATHER1 + s)
        block_l = g.at[s, y, c, :, :, halves[0]]
        block_r = g.at[s, :, c, x, :, halves[1]]
        for o in (2, 1, 3):
            copy_to(block_l, block_l, at_y(o), GATHER2 + s * 6 + o - 1)
            copy_to(block_r, block_r, at_x(o), GATHER2 + s * 6 + o + 2)
        for o in (1, 2, 3):
            piece = g.at[s, y, c, (x + o) % NX, :, halves[0]]
            copy_to(piece, piece, sibling, FORWARD + s)
            piece = g.at[s, (y + o) % NY, c, x, :, halves[1]]
            copy_to(piece, piece, sibling, FORWARD + s)

    def gather_end(s):
        for o in (1, 3, 2):
            block = g.at[s, (y + 4 - o) % NY, c, :, :, halves[0]]
            arrived(block, GATHER2 + s * 6 + o - 1)
            copy_to(block, block, sibling, FORWARD + s)
            block = g.at[s, :, c, (x + 4 - o) % NX, :, halves[1]]
            arrived(block, GATHER2 + s * 6 + o + 2)
            copy_to(block, block, sibling, FORWARD + s)

    low = lax.broadcasted_iota(jnp.int32, (32, 128), 1) < 64

    def output_terms(s, core):
        if core == 0:
            if s == 0:
                loads["wo"].wait()
                loads["wo2"].wait()
        else:
            arrived(g.at[s, :, 1 - c], FORWARD + s)
        core = c if core == 0 else 1 - c
        terms = dot_nt(g[s, :, core].reshape(256, COLS), vwo[...])
        for yy in range(NY):
            mine = terms[yy * 64:(yy + 1) * 64]
            for cb in range(4):
                for half in range(2):
                    zpart[s, yy, core, 2 * cb + half] = mine[
                        half * 32:(half + 1) * 32, cb * 128:(cb + 1) * 128
                    ]
            zpart[s, yy, core, 8] = jnp.where(low, mine[:32, 512:640], mine[32:, 512:640])

    ends = {}
    pieces = (pl.ds(0, 5), pl.ds(5, 4))

    def ring_sem(s, way, step, sub):
        return RING + ((s * 2 + way) * 4 + step) * 2 + sub

    def ring_add(s, way, step, sub, first):
        dest = (z + 4 - step) % NZ if way == 0 else (z + 4 + step) % NZ
        total = zpart[s, dest // 2, dest % 2, pieces[sub]]
        if not first:
            arrived(zr.at[s, way, step - 1, pieces[sub]], ring_sem(s, way, step - 1, sub))
            total = total + zr[s, way, step - 1, pieces[sub]].astype(F32)
        zs[s, way, step, pieces[sub]] = total.astype(BF)
        copy_to(
            zs.at[s, way, step, pieces[sub]], zr.at[s, way, step, pieces[sub]],
            at_z(1 if way == 0 else 7), ring_sem(s, way, step, sub),
        )

    def ring_start(s):
        for way in range(2):
            ring_add(s, way, 0, way, True)
        for way in range(2):
            ring_add(s, way, 1, 1 - way, True)

    def ring_step(s, step, late):
        for way in range(2):
            ring_add(s, way, step, way if late else 1 - way, False)

    def ring_end(s):
        for way in range(2):
            for sub in range(2):
                arrived(zr.at[s, way, 3, pieces[sub]], ring_sem(s, way, 3, sub))
        total = zpart[s, z // 2, z % 2] + zr[s, 0, 3].astype(F32) + zr[s, 1, 3].astype(F32)
        ends[s] = total.astype(BF)

    steps = [
        (swap_unit, 0), (swap_unit, 1), (start_unit, 0), (start_unit, 1),
        (swap_unit, 2), (swap_unit, 3), (start_unit, 2), (start_unit, 3),
        (middle_unit, 0), (middle_unit, 1), (middle_unit, 2), (middle_unit, 3),
        (send_queries, 0), (send_queries, 1), (attention, 0), (attention, 1),
        (gather_start, 0), (gather_start, 1), (gather_middle, 0), (gather_middle, 1),
        (gather_end, 0), (output_terms, 0, 0), (output_terms, 0, 1), (ring_start, 0),
        (gather_end, 1), (output_terms, 1, 0), (output_terms, 1, 1), (ring_start, 1),
        (ring_step, 0, 1, True), (ring_step, 0, 2, False),
        (ring_step, 1, 1, True), (ring_step, 1, 2, False),
        (ring_step, 0, 2, True), (ring_step, 0, 3, False),
        (ring_step, 1, 2, True), (ring_step, 1, 3, False),
        (ring_step, 0, 3, True), (ring_step, 1, 3, True),
        (ring_end, 0), (ring_end, 1),
    ]
    for function, *arguments in steps:
        function(*arguments)
    first, second = ends[0], ends[1]

    from_row = (k == ((r >> 1) & 1) * 64 + ((r >> 2) & 3) * 16 + (r >> 4) * 2 + (r & 1))
    to_rows = one_hot(from_row)
    for cb in range(4):
        both = jnp.concatenate(
            [first[2 * cb:2 * cb + 2].reshape(64, 128), second[2 * cb:2 * cb + 2].reshape(64, 128)], axis=0
        )
        out[:, cb * 128:(cb + 1) * 128] = dot_nn(to_rows, both).astype(BF)
    tails = jnp.concatenate([first[8], first[8], second[8], second[8]], axis=0)
    in_low = one_hot(from_row & ((k & 32) == 0))
    in_high = one_hot(from_row & ((k & 32) != 0))
    tail = dot_nn(in_low, tails) + pltpu.roll(dot_nn(in_high, tails), 64, 1)
    out[:, 512:576] = tail[:, :64].astype(BF)

    for copy in slots:
        copy.wait_send()


def local(tokens, w_query, w_keyval, w_out, cache_keys, cache_values, lengths):
    vm = pltpu.VMEM
    units = (LEFT, RIGHT, LEFT, RIGHT)
    scratch = [
        vm((2, D_LOC, 512), BF), vm((D_LOC, COLS), BF), vm((128, D_LOC), BF), vm((640, COLS), BF),
        vm((2, SLOTS, HD), BF), vm((2, SLOTS, HD), BF), pltpu.SMEM((2,), jnp.int32), vm((2, 2, 256, D_LOC), BF),
        vm((2, 256, LEFT + RIGHT), BF), vm((2, 256, LEFT + RIGHT), BF),
        *[vm((4, 4, 16, w), BF) for w in units],
        *[vm((3, 4, 16, w), BF) for w in units],
        *[vm((4, 16, w), BF) for w in units],
        *[vm((3, 16, w), BF) for w in units],
        vm((2, 128, HD), BF),
        *[vm((2, NZ, 16, HD), BF) for _ in range(4)],
        vm((2, NY, 2, NX, 16, COLS), BF),
        vm((2, NY, 2, 9, 32, 128), F32),
        vm((2, 2, 4, 9, 32, 128), BF), vm((2, 2, 4, 9, 32, 128), BF),
        pltpu.SemaphoreType.DMA((8,)), pltpu.SemaphoreType.DMA((SEND_SLOTS,)), pltpu.SemaphoreType.DMA((RING + 32,)),
    ]
    hbm = pl.BlockSpec(memory_space=pl.ANY)
    result = pl.pallas_call(
        kernel,
        out_shape=jax.ShapeDtypeStruct((128, D_LOC), BF),
        in_specs=[hbm] * 7,
        out_specs=pl.BlockSpec(memory_space=pltpu.VMEM),
        scratch_shapes=scratch,
        compiler_params=pltpu.CompilerParams(
            collective_id=0, has_side_effects=True, vmem_limit_bytes=56 * 2**20
        ),
        cost_estimate=pl.CostEstimate(flops=4 * 10**9, bytes_accessed=10**7, transcendentals=10**6),
        name="layer",
    )(
        tokens.transpose(1, 2, 0), w_query, w_keyval.T, w_out.T, cache_keys, cache_values, lengths
    )
    return result.reshape(64, 2, D_LOC)


def solution(mesh):
    placed = (
        P(None, None, ("batch", "gy")),
        P(("batch", "gy"), "gx"),
        P(("batch", "gy"), "gx"),
        P("gx", ("batch", "gy")),
        P(("batch", "gx", "gy"), None, None),
        P(("batch", "gx", "gy"), None, None),
        P(("batch", "gx", "gy")),
    )
    return jax.shard_map(
        local, mesh=mesh, in_specs=placed, out_specs=P("gx", None, ("batch", "gy")), check_vma=False
    )
```

```python
import functools

import jax
import jax.numpy as jnp
import numpy as np
from jax import lax
from jax.experimental import pallas as pl
from jax.experimental.pallas import tpu as pltpu
from jax.sharding import PartitionSpec as P

MESH = pl.DeviceIdType.MESH
BF = jnp.bfloat16
F32 = jnp.float32
NX, NY, NZ = 4, 4, 8
D_LOC, COLS = 576, 1536
HD, SLOTS = 256, 2048
SEND_SLOTS = 40
SWAP, STAGE1, STAGE2, QUERIES, RESULTS, GATHER1, FORWARD, GATHER2, RING, RELAY = 0, 4, 8, 12, 14, 16, 28, 30, 42, 74
RELAYED = (0, 1, 2, 3)
LEFT, RIGHT = 768, 896


def dot_nt(a, b):
    return lax.dot_general(a, b, (((1,), (1,)), ((), ())), preferred_element_type=F32)


def dot_nn(a, b):
    return lax.dot_general(a, b, (((1,), (0,)), ((), ())), preferred_element_type=F32)


def grid_of(rows, cols):
    return (
        lax.broadcasted_iota(jnp.int32, (rows, cols), 0),
        lax.broadcasted_iota(jnp.int32, (rows, cols), 1),
    )


def one_hot(hit):
    return jnp.where(hit, 1.0, 0.0).astype(BF)


def kernel(
    tok, wq, wkv, wo, ck, cv, lens_in, out,
    vtok, vwq, vwkv, vwo, vk, vv, lens, xp,
    sib_s, sib_r, part0, part1, part2, part3, got0, got1, got2, got3,
    mid0, mid1, mid2, mid3, fin0, fin1, fin2, fin3,
    stack, qs, qr, ats, atr, g, zpart, zs, zr,
    ld_sem, send_sem, recv_sem,
):
    b = lax.axis_index("batch")
    z = lax.axis_index("gx")
    x = lax.axis_index("gy")
    y, c = b // 2, b % 2

    loads = {}
    for k, (name, src, dst) in enumerate([
        ("tok", tok, vtok),
        ("wq", wq, vwq),
        ("wkv", wkv, vwkv.at[pl.ds(0, 64)]),
        ("lens", lens_in, lens),
        ("k", ck, vk),
        ("v", cv, vv),
        ("wo", wo, vwo.at[pl.ds(0, D_LOC)]),
        ("wo2", wo.at[pl.ds(512, 64)], vwo.at[pl.ds(D_LOC, 64)]),
    ]):
        loads[name] = pltpu.make_async_copy(src, dst, ld_sem.at[k])
        loads[name].start()

    def at_x(o):
        return (b, z, (x + o) % NX)

    def at_y(o):
        return ((b + 2 * o) % (2 * NY), z, x)

    def at_z(o):
        return (b, (z + o) % NZ, x)

    sibling = (y * 2 + (1 - c), z, x)

    barrier = pltpu.get_barrier_semaphore()
    partners = [sibling] + [at_x(o) for o in (1, 2, 3)] + [at_y(o) for o in (1, 2, 3)]
    partners += [at_z(o) for o in range(1, NZ)]
    for partner in partners:
        pl.semaphore_signal(barrier, inc=1, device_id=partner, device_id_type=MESH)

    slots = [None] * SEND_SLOTS
    count = [0]

    def copy_to(src, dst, device, sem):
        k = count[0] % SEND_SLOTS
        count[0] += 1
        if slots[k] is not None:
            slots[k].wait_send()
        copy = pltpu.make_async_remote_copy(
            src_ref=src, dst_ref=dst, send_sem=send_sem.at[k], recv_sem=recv_sem.at[sem],
            device_id=device, device_id_type=MESH,
        )
        copy.start()
        slots[k] = copy

    def arrived(ref, sem):
        pltpu.make_async_copy(ref, ref, recv_sem.at[sem]).wait()

    vwkv[64:128, :] = jnp.zeros((64, D_LOC), BF)
    r, k = grid_of(256, 256)
    perm = one_hot(
        k == (r & 1) * 128 + ((r >> 6) & 1) * 64 + ((r >> 1) & 7) * 8 + ((r >> 4) & 3) * 2 + (r >> 7)
    )
    loads["tok"].wait()
    for yy in range(NY):
        both = jnp.concatenate(
            [vtok[0, :, yy * 128:(yy + 1) * 128], vtok[1, :, yy * 128:(yy + 1) * 128]], axis=1
        )
        rows = dot_nt(perm, both).astype(BF)
        for s in range(2):
            for cc in range(2):
                at = (s * 2 + cc) * 64
                xp[s, cc, yy * 64:(yy + 1) * 64, :] = rows[at:at + 64]
    loads["wq"].wait()
    loads["wkv"].wait()

    first_two, last_two = pl.ds(0, 2), pl.ds(2, 2)
    parts, gots = (part0, part1, part2, part3), (got0, got1, got2, got3)
    mids, fins = (mid0, mid1, mid2, mid3), (fin0, fin1, fin2, fin3)
    first_x = (True, False, False, True)

    def project(s, side, core):
        rows = xp[s, core]
        if side == 0:
            return dot_nn(rows, vwq[:, 0:LEFT])
        return jnp.concatenate([dot_nn(rows, vwq[:, LEFT:COLS]), dot_nt(rows, vwkv[...])], axis=1)

    def width(side):
        return LEFT if side == 0 else RIGHT

    def cols_of(side):
        return pl.ds(0, LEFT) if side == 0 else pl.ds(LEFT, RIGHT)

    def swap_unit(u):
        s, side = divmod(u, 2)
        cols = cols_of(side)
        sib_s[s, :, cols] = project(s, side, 1 - c).astype(BF)
        if u == 0:
            pl.semaphore_wait(barrier, len(partners))
        copy_to(sib_s.at[s, :, cols], sib_r.at[s, :, cols], sibling, SWAP + u)

    def start_unit(u):
        s, side = divmod(u, 2)
        cols = cols_of(side)
        own = project(s, side, c)
        arrived(sib_r.at[s, :, cols], SWAP + u)
        total = (own + sib_r[s, :, cols].astype(F32)).astype(BF)
        for yy in range(NY):
            for xx in range(NX):
                at = (yy * NX + xx) * 16
                lead = (xx, yy) if first_x[u] else (yy, xx)
                parts[u][lead[0], lead[1]] = total[at:at + 16]
        me, to = (x, at_x) if first_x[u] else (y, at_y)
        if u not in RELAYED:
            for o in (2, 1, 3):
                copy_to(parts[u].at[(me + o) % 4], gots[u].at[o - 1], to(o), STAGE1 + u)
            return
        ahead, far, behind = (me + 1) % 4, (me + 2) % 4, (me + 3) % 4
        copy_to(parts[u].at[far, first_two], gots[u].at[2, first_two], to(1), RELAY + 2 * u)
        copy_to(parts[u].at[far, last_two], gots[u].at[2, last_two], to(3), RELAY + 2 * u + 1)
        copy_to(parts[u].at[ahead, last_two], gots[u].at[0, last_two], to(1), STAGE1 + u)
        copy_to(parts[u].at[behind, first_two], gots[u].at[1, first_two], to(3), STAGE1 + u)

    def relay_unit(u):
        me, to = (x, at_x) if first_x[u] else (y, at_y)
        for way, half, o in ((0, first_two, 1), (1, last_two, 3)):
            arrived(gots[u].at[2, half], RELAY + 2 * u + way)
            mine = parts[u].at[(me + o) % 4, half]
            mine[...] = (mine[...].astype(F32) + gots[u][2, half].astype(F32)).astype(BF)
            copy_to(mine, gots[u].at[way, half], to(o), STAGE1 + u)

    def middle_unit(u):
        me, to, other = (x, at_y, y) if first_x[u] else (y, at_x, x)
        came = 2 if u in RELAYED else 3
        arrived(gots[u].at[pl.ds(0, came)], STAGE1 + u)
        total = parts[u][me].astype(F32)
        for o in range(came):
            total = total + gots[u][o].astype(F32)
        mids[u][...] = total.astype(BF)
        for o in (2, 1, 3):
            copy_to(mids[u].at[(other + o) % 4], fins[u].at[o - 1], to(o), STAGE2 + u)

    def finish_unit(u):
        other = y if first_x[u] else x
        arrived(fins[u], STAGE2 + u)
        total = mids[u][other].astype(F32)
        for o in range(3):
            total = total + fins[u][o].astype(F32)
        return total.astype(BF)

    r, k = grid_of(128, 128)
    slot = r & 15
    to_groups = one_hot((slot < 14) & (k == (slot >> 1) * 16 + (r >> 4) * 2 + (slot & 1)))
    r, k = grid_of(128, 256)
    place = one_hot((r < 64) & (k == r + (z % 4) * 64))

    def send_queries(s):
        left = finish_unit(2 * s)
        right = finish_unit(2 * s + 1)
        for h in range(3):
            stack[s, h * 16:(h + 1) * 16] = left[:, h * HD:(h + 1) * HD]
            stack[s, (h + 3) * 16:(h + 4) * 16] = right[:, h * HD:(h + 1) * HD]
        stack[s, 96:112] = dot_nn(right[:, LEFT:RIGHT], place).astype(BF)
        stack[s, 112:128] = jnp.zeros((16, HD), BF)
        grouped = dot_nn(to_groups, stack[s]).astype(BF)
        for zz in range(NZ):
            qs[s, zz] = grouped[zz * 16:(zz + 1) * 16]
        for o in (4, 3, 5, 2, 6, 1, 7):
            copy_to(qs.at[s, (z + o) % NZ], qr.at[s, z], at_z(o), QUERIES + s)
        qr[s, z] = qs[s, z]

    loads["lens"].wait()
    r, k = grid_of(8, 128)
    freqs = jnp.exp(k.astype(F32) * (-np.log(10000.0) / 128))
    length = jnp.where((r & 2) == 0, lens[0], lens[1])
    angle = (length + (r & 1)).astype(F32) * freqs
    cosine, sine = jnp.cos(angle), jnp.sin(angle)

    r, k = grid_of(128, 128)
    pick_key = one_hot((r < 2) & ((k & 15) == 12 + r) & ((k >> 4) < 4))
    pick_value = one_hot((r < 2) & ((k & 15) == 12 + r) & ((k >> 4) >= 4))
    odd = (r & 1) == 1
    causal = k <= (r & 1)

    def attention(s):
        arrived(qr.at[s, pl.ds(0, NZ - 1)], QUERIES + s)
        raw = qr[s].reshape(128, HD)
        cos_rows = jnp.where(odd, cosine[2 * s + 1:2 * s + 2], cosine[2 * s:2 * s + 1])
        sin_rows = jnp.where(odd, sine[2 * s + 1:2 * s + 2], sine[2 * s:2 * s + 1])

        def rotate(values):
            u, w = values[:, :128], values[:, 128:]
            return jnp.concatenate(
                [u * cos_rows - w * sin_rows, w * cos_rows + u * sin_rows], axis=1
            ).astype(BF)

        queries = rotate(raw.astype(F32))
        new_keys = rotate(dot_nn(pick_key, raw))
        new_values = dot_nn(pick_value, raw).astype(BF)
        if s == 0:
            loads["k"].wait()
        scale = 1.0 / HD**0.5
        cached = dot_nt(queries, vk[s]) * scale
        _, column = grid_of(128, SLOTS)
        cached = jnp.where(column < lens[s], cached, -1e30)
        fresh = jnp.where(causal, dot_nt(queries, new_keys) * scale, -1e30)
        highest = jnp.maximum(cached.max(-1, keepdims=True), fresh.max(-1, keepdims=True))
        cached = jnp.exp(cached - highest)
        fresh = jnp.exp(fresh - highest)
        denom = cached.sum(-1, keepdims=True) + fresh.sum(-1, keepdims=True)
        if s == 0:
            loads["v"].wait()
        result = dot_nn(cached.astype(BF), vv[s]) + dot_nn(fresh.astype(BF), new_values)
        result = (result / denom).astype(BF)
        for zz in range(NZ):
            ats[s, zz] = result[zz * 16:(zz + 1) * 16]
        for o in (4, 3, 5, 2, 6, 1, 7):
            copy_to(ats.at[s, (z + o) % NZ], atr.at[s, z], at_z(o), RESULTS + s)
        atr[s, z] = ats[s, z]

    halves = (pl.ds(0, COLS // 2), pl.ds(COLS // 2, COLS // 2))
    to_heads = one_hot((r < 96) & (k == ((r >> 1) & 7) * 16 + (r >> 4) * 2 + (r & 1)))

    def gather_start(s):
        arrived(atr.at[s, pl.ds(0, NZ - 1)], RESULTS + s)
        heads = dot_nn(to_heads, atr[s].reshape(128, HD)).astype(BF)
        for h in range(6):
            g[s, y, c, x, :, h * HD:(h + 1) * HD] = heads[h * 16:(h + 1) * 16]
        mine_l = g.at[s, y, c, x, :, halves[0]]
        mine_r = g.at[s, y, c, x, :, halves[1]]
        for o in (2, 1, 3):
            copy_to(mine_l, mine_l, at_x(o), GATHER1 + s * 6 + o - 1)
            copy_to(mine_r, mine_r, at_y(o), GATHER1 + s * 6 + o + 2)
        copy_to(g.at[s, y, c, x], g.at[s, y, c, x], sibling, FORWARD + s)
        for o in (2, 1, 3):
            copy_to(mine_l, mine_l, at_y(o), GATHER2 + s * 6 + o - 1)
            copy_to(mine_r, mine_r, at_x(o), GATHER2 + s * 6 + o + 2)

    def gather_middle(s):
        for come in (1, 3, 2):
            piece_l = g.at[s, y, c, (x + 4 - come) % NX, :, halves[0]]
            piece_r = g.at[s, (y + 4 - come) % NY, c, x, :, halves[1]]
            arrived(piece_l, GATHER1 + s * 6 + come - 1)
            for o in (2, 1, 3):
                copy_to(piece_l, piece_l, at_y(o), GATHER2 + s * 6 + o - 1)
            copy_to(piece_l, piece_l, sibling, FORWARD + s)
            arrived(piece_r, GATHER1 + s * 6 + come + 2)
            for o in (2, 1, 3):
                copy_to(piece_r, piece_r, at_x(o), GATHER2 + s * 6 + o + 2)
            copy_to(piece_r, piece_r, sibling, FORWARD + s)

    def gather_end(s):
        for o in (1, 3, 2):
            block = g.at[s, (y + 4 - o) % NY, c, :, :, halves[0]]
            arrived(block, GATHER2 + s * 6 + o - 1)
            copy_to(block, block, sibling, FORWARD + s)
            block = g.at[s, :, c, (x + 4 - o) % NX, :, halves[1]]
            arrived(block, GATHER2 + s * 6 + o + 2)
            copy_to(block, block, sibling, FORWARD + s)

    low = lax.broadcasted_iota(jnp.int32, (32, 128), 1) < 64

    def output_terms(s, core):
        if core == 0:
            if s == 0:
                loads["wo"].wait()
                loads["wo2"].wait()
        else:
            arrived(g.at[s, :, 1 - c], FORWARD + s)
        core = c if core == 0 else 1 - c
        terms = dot_nt(g[s, :, core].reshape(256, COLS), vwo[...])
        for yy in range(NY):
            mine = terms[yy * 64:(yy + 1) * 64]
            for cb in range(4):
                for half in range(2):
                    zpart[s, yy, core, 2 * cb + half] = mine[
                        half * 32:(half + 1) * 32, cb * 128:(cb + 1) * 128
                    ]
            zpart[s, yy, core, 8] = jnp.where(low, mine[:32, 512:640], mine[32:, 512:640])

    ends = {}
    pieces = (pl.ds(0, 5), pl.ds(5, 4))

    def ring_sem(s, way, step, sub):
        return RING + ((s * 2 + way) * 4 + step) * 2 + sub

    def ring_add(s, way, step, sub, first):
        dest = (z + 4 - step) % NZ if way == 0 else (z + 4 + step) % NZ
        total = zpart[s, dest // 2, dest % 2, pieces[sub]]
        if not first:
            arrived(zr.at[s, way, step - 1, pieces[sub]], ring_sem(s, way, step - 1, sub))
            total = total + zr[s, way, step - 1, pieces[sub]].astype(F32)
        zs[s, way, step, pieces[sub]] = total.astype(BF)
        copy_to(
            zs.at[s, way, step, pieces[sub]], zr.at[s, way, step, pieces[sub]],
            at_z(1 if way == 0 else 7), ring_sem(s, way, step, sub),
        )

    def ring_start(s):
        for way in range(2):
            ring_add(s, way, 0, way, True)
        for way in range(2):
            ring_add(s, way, 1, 1 - way, True)

    def ring_step(s, step, late):
        for way in range(2):
            ring_add(s, way, step, way if late else 1 - way, False)

    def ring_end(s):
        for way in range(2):
            for sub in range(2):
                arrived(zr.at[s, way, 3, pieces[sub]], ring_sem(s, way, 3, sub))
        total = zpart[s, z // 2, z % 2] + zr[s, 0, 3].astype(F32) + zr[s, 1, 3].astype(F32)
        ends[s] = total.astype(BF)

    steps = [
        (swap_unit, 0),
        (swap_unit, 1),
        (start_unit, 0),
        (start_unit, 1),
        (swap_unit, 3),
        (swap_unit, 2),
        (start_unit, 3),
        (start_unit, 2),
        (relay_unit, 0),
        (relay_unit, 1),
        (relay_unit, 3),
        (relay_unit, 2),
        (middle_unit, 0),
        (middle_unit, 1),
        (middle_unit, 3),
        (middle_unit, 2),
        (send_queries, 0),
        (send_queries, 1),
        (attention, 0),
        (attention, 1),
        (gather_start, 0),
        (gather_start, 1),
        (gather_middle, 0),
        (gather_middle, 1),
        (gather_end, 0),
        (output_terms, 0, 0),
        (output_terms, 0, 1),
        (ring_start, 0),
        (gather_end, 1),
        (output_terms, 1, 0),
        (output_terms, 1, 1),
        (ring_start, 1),
        (ring_step, 0, 1, True),
        (ring_step, 0, 2, False),
        (ring_step, 1, 1, True),
        (ring_step, 1, 2, False),
        (ring_step, 0, 2, True),
        (ring_step, 0, 3, False),
        (ring_step, 1, 2, True),
        (ring_step, 1, 3, False),
        (ring_step, 0, 3, True),
        (ring_step, 1, 3, True),
        (ring_end, 0),
        (ring_end, 1),
    ]
    for function, *arguments in steps:
        function(*arguments)
    first, second = ends[0], ends[1]

    from_row = (k == ((r >> 1) & 1) * 64 + ((r >> 2) & 3) * 16 + (r >> 4) * 2 + (r & 1))
    to_rows = one_hot(from_row)
    for cb in range(4):
        both = jnp.concatenate(
            [first[2 * cb:2 * cb + 2].reshape(64, 128), second[2 * cb:2 * cb + 2].reshape(64, 128)], axis=0
        )
        out[:, cb * 128:(cb + 1) * 128] = dot_nn(to_rows, both).astype(BF)
    tails = jnp.concatenate([first[8], first[8], second[8], second[8]], axis=0)
    in_low = one_hot(from_row & ((k & 32) == 0))
    in_high = one_hot(from_row & ((k & 32) != 0))
    tail = dot_nn(in_low, tails) + pltpu.roll(dot_nn(in_high, tails), 64, 1)
    out[:, 512:576] = tail[:, :64].astype(BF)

    for copy in slots:
        copy.wait_send()


def local(tokens, w_query, w_keyval, w_out, cache_keys, cache_values, lengths):
    vm = pltpu.VMEM
    units = (LEFT, RIGHT, LEFT, RIGHT)
    scratch = [
        vm((2, D_LOC, 512), BF), vm((D_LOC, COLS), BF), vm((128, D_LOC), BF), vm((640, COLS), BF),
        vm((2, SLOTS, HD), BF), vm((2, SLOTS, HD), BF), pltpu.SMEM((2,), jnp.int32), vm((2, 2, 256, D_LOC), BF),
        vm((2, 256, LEFT + RIGHT), BF), vm((2, 256, LEFT + RIGHT), BF),
        *[vm((4, 4, 16, w), BF) for w in units],
        *[vm((3, 4, 16, w), BF) for w in units],
        *[vm((4, 16, w), BF) for w in units],
        *[vm((3, 16, w), BF) for w in units],
        vm((2, 128, HD), BF),
        *[vm((2, NZ, 16, HD), BF) for _ in range(4)],
        vm((2, NY, 2, NX, 16, COLS), BF),
        vm((2, NY, 2, 9, 32, 128), F32),
        vm((2, 2, 4, 9, 32, 128), BF), vm((2, 2, 4, 9, 32, 128), BF),
        pltpu.SemaphoreType.DMA((8,)), pltpu.SemaphoreType.DMA((SEND_SLOTS,)), pltpu.SemaphoreType.DMA((RELAY + 8,)),
    ]
    hbm = pl.BlockSpec(memory_space=pl.ANY)
    result = pl.pallas_call(
        kernel,
        out_shape=jax.ShapeDtypeStruct((128, D_LOC), BF),
        in_specs=[hbm] * 7,
        out_specs=pl.BlockSpec(memory_space=pltpu.VMEM),
        scratch_shapes=scratch,
        compiler_params=pltpu.CompilerParams(
            collective_id=0, has_side_effects=True, vmem_limit_bytes=56 * 2**20
        ),
        cost_estimate=pl.CostEstimate(flops=4 * 10**9, bytes_accessed=10**7, transcendentals=10**6),
        name="layer",
    )(
        tokens.transpose(1, 2, 0), w_query, w_keyval.T, w_out.T, cache_keys, cache_values, lengths
    )
    return result.reshape(64, 2, D_LOC)


def solution(mesh):
    placed = (
        P(None, None, ("batch", "gy")),
        P(("batch", "gy"), "gx"),
        P(("batch", "gy"), "gx"),
        P("gx", ("batch", "gy")),
        P(("batch", "gx", "gy"), None, None),
        P(("batch", "gx", "gy"), None, None),
        P(("batch", "gx", "gy")),
    )
    return jax.shard_map(
        local, mesh=mesh, in_specs=placed, out_specs=P("gx", None, ("batch", "gy")), check_vma=False
    )
```

```python
import functools

import jax
import jax.numpy as jnp
import numpy as np
from jax import lax
from jax.experimental import pallas as pl
from jax.experimental.pallas import tpu as pltpu
from jax.sharding import PartitionSpec as P

MESH = pl.DeviceIdType.MESH
BF = jnp.bfloat16
F32 = jnp.float32
NX, NY, NZ = 4, 4, 8
D_LOC, COLS = 576, 1536
HD, SLOTS = 256, 2048
SEND_SLOTS = 28
SWAP, STAGE1, STAGE2, QUERIES, RESULTS, GATHER1, FORWARD, GATHER2, RING, RELAY = 0, 4, 8, 12, 14, 16, 28, 30, 42, 74
RELAYED = (0, 1, 2, 3)
LEFT, RIGHT = 768, 896


def dot_nt(a, b):
    return lax.dot_general(a, b, (((1,), (1,)), ((), ())), preferred_element_type=F32)


def dot_nn(a, b):
    return lax.dot_general(a, b, (((1,), (0,)), ((), ())), preferred_element_type=F32)


def grid_of(rows, cols):
    return (
        lax.broadcasted_iota(jnp.int32, (rows, cols), 0),
        lax.broadcasted_iota(jnp.int32, (rows, cols), 1),
    )


def one_hot(hit):
    return jnp.where(hit, 1.0, 0.0).astype(BF)


def kernel(
    tok, wq, wkv, wo, ck, cv, lens_in, out,
    vtok, vwq, vwkv, vwo, vk, vv, lens, xp,
    sib_s, sib_r, part0, part1, part2, part3, got0, got1, got2, got3,
    mid0, mid1, mid2, mid3, fin0, fin1, fin2, fin3,
    stack, qs, qr, ats, atr, g, zpart, zs, zr,
    ld_sem, send_sem, recv_sem,
):
    b = lax.axis_index("batch")
    z = lax.axis_index("gx")
    x = lax.axis_index("gy")
    y, c = b // 2, b % 2

    loads = {}
    for k, (name, src, dst) in enumerate([
        ("tok", tok, vtok),
        ("wq", wq, vwq),
        ("wkv", wkv, vwkv.at[pl.ds(0, 64)]),
        ("lens", lens_in, lens),
        ("k", ck, vk),
        ("v", cv, vv),
        ("wo", wo, vwo.at[pl.ds(0, D_LOC)]),
        ("wo2", wo.at[pl.ds(512, 64)], vwo.at[pl.ds(D_LOC, 64)]),
    ]):
        loads[name] = pltpu.make_async_copy(src, dst, ld_sem.at[k])
        loads[name].start()

    def at_x(o):
        return (b, z, (x + o) % NX)

    def at_y(o):
        return ((b + 2 * o) % (2 * NY), z, x)

    def at_z(o):
        return (b, (z + o) % NZ, x)

    sibling = (y * 2 + (1 - c), z, x)

    barrier = pltpu.get_barrier_semaphore()
    partners = [sibling] + [at_x(o) for o in (1, 2, 3)] + [at_y(o) for o in (1, 2, 3)]
    partners += [at_z(o) for o in range(1, NZ)]
    for partner in partners:
        pl.semaphore_signal(barrier, inc=1, device_id=partner, device_id_type=MESH)

    slots = [None] * SEND_SLOTS
    count = [0]

    def copy_to(src, dst, device, sem):
        k = count[0] % SEND_SLOTS
        count[0] += 1
        if slots[k] is not None:
            slots[k].wait_send()
        copy = pltpu.make_async_remote_copy(
            src_ref=src, dst_ref=dst, send_sem=send_sem.at[k], recv_sem=recv_sem.at[sem],
            device_id=device, device_id_type=MESH,
        )
        copy.start()
        slots[k] = copy

    def arrived(ref, sem):
        pltpu.make_async_copy(ref, ref, recv_sem.at[sem]).wait()

    vwkv[64:128, :] = jnp.zeros((64, D_LOC), BF)
    r, k = grid_of(256, 256)
    perm = one_hot(
        k == (r & 1) * 128 + ((r >> 6) & 1) * 64 + ((r >> 1) & 7) * 8 + ((r >> 4) & 3) * 2 + (r >> 7)
    )
    loads["tok"].wait()
    for yy in range(NY):
        both = jnp.concatenate(
            [vtok[0, :, yy * 128:(yy + 1) * 128], vtok[1, :, yy * 128:(yy + 1) * 128]], axis=1
        )
        rows = dot_nt(perm, both).astype(BF)
        for s in range(2):
            for cc in range(2):
                at = (s * 2 + cc) * 64
                xp[s, cc, yy * 64:(yy + 1) * 64, :] = rows[at:at + 64]
    loads["wq"].wait()
    loads["wkv"].wait()

    first_two, last_two = pl.ds(0, 2), pl.ds(2, 2)
    parts, gots = (part0, part1, part2, part3), (got0, got1, got2, got3)
    mids, fins = (mid0, mid1, mid2, mid3), (fin0, fin1, fin2, fin3)
    first_x = (True, False, False, True)

    def project(s, side, core):
        rows = xp[s, core]
        if side == 0:
            return dot_nn(rows, vwq[:, 0:LEFT])
        return jnp.concatenate([dot_nn(rows, vwq[:, LEFT:COLS]), dot_nt(rows, vwkv[...])], axis=1)

    def width(side):
        return LEFT if side == 0 else RIGHT

    def cols_of(side):
        return pl.ds(0, LEFT) if side == 0 else pl.ds(LEFT, RIGHT)

    def swap_unit(u):
        s, side = divmod(u, 2)
        cols = cols_of(side)
        sib_s[s, :, cols] = project(s, side, 1 - c).astype(BF)
        if u == 0:
            pl.semaphore_wait(barrier, len(partners))
        copy_to(sib_s.at[s, :, cols], sib_r.at[s, :, cols], sibling, SWAP + u)

    def start_unit(u):
        s, side = divmod(u, 2)
        cols = cols_of(side)
        own = project(s, side, c)
        arrived(sib_r.at[s, :, cols], SWAP + u)
        total = (own + sib_r[s, :, cols].astype(F32)).astype(BF)
        for yy in range(NY):
            for xx in range(NX):
                at = (yy * NX + xx) * 16
                lead = (xx, yy) if first_x[u] else (yy, xx)
                parts[u][lead[0], lead[1]] = total[at:at + 16]
        me, to = (x, at_x) if first_x[u] else (y, at_y)
        if u not in RELAYED:
            for o in (2, 1, 3):
                copy_to(parts[u].at[(me + o) % 4], gots[u].at[o - 1], to(o), STAGE1 + u)
            return
        ahead, far, behind = (me + 1) % 4, (me + 2) % 4, (me + 3) % 4
        copy_to(parts[u].at[far, first_two], gots[u].at[2, first_two], to(1), RELAY + 2 * u)
        copy_to(parts[u].at[far, last_two], gots[u].at[2, last_two], to(3), RELAY + 2 * u + 1)
        copy_to(parts[u].at[ahead, last_two], gots[u].at[0, last_two], to(1), STAGE1 + u)
        copy_to(parts[u].at[behind, first_two], gots[u].at[1, first_two], to(3), STAGE1 + u)

    def relay_unit(u):
        me, to = (x, at_x) if first_x[u] else (y, at_y)
        for way, half, o in ((0, first_two, 1), (1, last_two, 3)):
            arrived(gots[u].at[2, half], RELAY + 2 * u + way)
            mine = parts[u].at[(me + o) % 4, half]
            mine[...] = (mine[...].astype(F32) + gots[u][2, half].astype(F32)).astype(BF)
            copy_to(mine, gots[u].at[way, half], to(o), STAGE1 + u)

    def middle_unit(u):
        me, to, other = (x, at_y, y) if first_x[u] else (y, at_x, x)
        came = 2 if u in RELAYED else 3
        arrived(gots[u].at[pl.ds(0, came)], STAGE1 + u)
        total = parts[u][me].astype(F32)
        for o in range(came):
            total = total + gots[u][o].astype(F32)
        mids[u][...] = total.astype(BF)
        for o in (2, 1, 3):
            copy_to(mids[u].at[(other + o) % 4], fins[u].at[o - 1], to(o), STAGE2 + u)

    def finish_unit(u):
        other = y if first_x[u] else x
        arrived(fins[u], STAGE2 + u)
        total = mids[u][other].astype(F32)
        for o in range(3):
            total = total + fins[u][o].astype(F32)
        return total.astype(BF)

    r, k = grid_of(128, 128)
    slot = r & 15
    to_groups = one_hot((slot < 14) & (k == (slot >> 1) * 16 + (r >> 4) * 2 + (slot & 1)))
    r, k = grid_of(128, 256)
    place = one_hot((r < 64) & (k == r + (z % 4) * 64))

    def send_queries(s):
        left = finish_unit(2 * s)
        right = finish_unit(2 * s + 1)
        for h in range(3):
            stack[s, h * 16:(h + 1) * 16] = left[:, h * HD:(h + 1) * HD]
            stack[s, (h + 3) * 16:(h + 4) * 16] = right[:, h * HD:(h + 1) * HD]
        stack[s, 96:112] = dot_nn(right[:, LEFT:RIGHT], place).astype(BF)
        stack[s, 112:128] = jnp.zeros((16, HD), BF)
        grouped = dot_nn(to_groups, stack[s]).astype(BF)
        for zz in range(NZ):
            qs[s, zz] = grouped[zz * 16:(zz + 1) * 16]
        for o in (4, 3, 5, 2, 6, 1, 7):
            copy_to(qs.at[s, (z + o) % NZ], qr.at[s, z], at_z(o), QUERIES + s)
        qr[s, z] = qs[s, z]

    loads["lens"].wait()
    r, k = grid_of(8, 128)
    freqs = jnp.exp(k.astype(F32) * (-np.log(10000.0) / 128))
    length = jnp.where((r & 2) == 0, lens[0], lens[1])
    angle = (length + (r & 1)).astype(F32) * freqs
    cosine, sine = jnp.cos(angle), jnp.sin(angle)

    r, k = grid_of(128, 128)
    pick_key = one_hot((r < 2) & ((k & 15) == 12 + r) & ((k >> 4) < 4))
    pick_value = one_hot((r < 2) & ((k & 15) == 12 + r) & ((k >> 4) >= 4))
    odd = (r & 1) == 1
    causal = k <= (r & 1)

    def attention(s):
        arrived(qr.at[s, pl.ds(0, NZ - 1)], QUERIES + s)
        raw = qr[s].reshape(128, HD)
        cos_rows = jnp.where(odd, cosine[2 * s + 1:2 * s + 2], cosine[2 * s:2 * s + 1])
        sin_rows = jnp.where(odd, sine[2 * s + 1:2 * s + 2], sine[2 * s:2 * s + 1])

        def rotate(values):
            u, w = values[:, :128], values[:, 128:]
            return jnp.concatenate(
                [u * cos_rows - w * sin_rows, w * cos_rows + u * sin_rows], axis=1
            ).astype(BF)

        queries = rotate(raw.astype(F32))
        new_keys = rotate(dot_nn(pick_key, raw))
        new_values = dot_nn(pick_value, raw).astype(BF)
        if s == 0:
            loads["k"].wait()
        scale = 1.0 / HD**0.5
        cached = dot_nt(queries, vk[s]) * scale
        _, column = grid_of(128, SLOTS)
        cached = jnp.where(column < lens[s], cached, -1e30)
        fresh = jnp.where(causal, dot_nt(queries, new_keys) * scale, -1e30)
        highest = jnp.maximum(cached.max(-1, keepdims=True), fresh.max(-1, keepdims=True))
        cached = jnp.exp(cached - highest)
        fresh = jnp.exp(fresh - highest)
        denom = cached.sum(-1, keepdims=True) + fresh.sum(-1, keepdims=True)
        if s == 0:
            loads["v"].wait()
        result = dot_nn(cached.astype(BF), vv[s]) + dot_nn(fresh.astype(BF), new_values)
        result = (result / denom).astype(BF)
        for zz in range(NZ):
            ats[s, zz] = result[zz * 16:(zz + 1) * 16]
        for o in (4, 3, 5, 2, 6, 1, 7):
            copy_to(ats.at[s, (z + o) % NZ], atr.at[s, z], at_z(o), RESULTS + s)
        atr[s, z] = ats[s, z]

    halves = (pl.ds(0, COLS // 2), pl.ds(COLS // 2, COLS // 2))
    to_heads = one_hot((r < 96) & (k == ((r >> 1) & 7) * 16 + (r >> 4) * 2 + (r & 1)))

    def gather_start(s):
        arrived(atr.at[s, pl.ds(0, NZ - 1)], RESULTS + s)
        heads = dot_nn(to_heads, atr[s].reshape(128, HD)).astype(BF)
        for h in range(6):
            g[s, y, c, x, :, h * HD:(h + 1) * HD] = heads[h * 16:(h + 1) * 16]
        mine_l = g.at[s, y, c, x, :, halves[0]]
        mine_r = g.at[s, y, c, x, :, halves[1]]
        for o in (2, 1, 3):
            copy_to(mine_l, mine_l, at_x(o), GATHER1 + s * 6 + o - 1)
            copy_to(mine_r, mine_r, at_y(o), GATHER1 + s * 6 + o + 2)
        copy_to(g.at[s, y, c, x], g.at[s, y, c, x], sibling, FORWARD + s)
        for o in (2, 1, 3):
            copy_to(mine_l, mine_l, at_y(o), GATHER2 + s * 6 + o - 1)
            copy_to(mine_r, mine_r, at_x(o), GATHER2 + s * 6 + o + 2)

    def gather_middle(s):
        for come in (1, 2, 3):
            piece_l = g.at[s, y, c, (x + 4 - come) % NX, :, halves[0]]
            piece_r = g.at[s, (y + 4 - come) % NY, c, x, :, halves[1]]
            arrived(piece_l, GATHER1 + s * 6 + come - 1)
            for o in (2, 1, 3):
                copy_to(piece_l, piece_l, at_y(o), GATHER2 + s * 6 + o - 1)
            copy_to(piece_l, piece_l, sibling, FORWARD + s)
            arrived(piece_r, GATHER1 + s * 6 + come + 2)
            for o in (2, 1, 3):
                copy_to(piece_r, piece_r, at_x(o), GATHER2 + s * 6 + o + 2)
            copy_to(piece_r, piece_r, sibling, FORWARD + s)

    def gather_end(s):
        for o in (1, 3, 2):
            block = g.at[s, (y + 4 - o) % NY, c, :, :, halves[0]]
            arrived(block, GATHER2 + s * 6 + o - 1)
            copy_to(block, block, sibling, FORWARD + s)
            block = g.at[s, :, c, (x + 4 - o) % NX, :, halves[1]]
            arrived(block, GATHER2 + s * 6 + o + 2)
            copy_to(block, block, sibling, FORWARD + s)

    low = lax.broadcasted_iota(jnp.int32, (32, 128), 1) < 64

    def output_terms(s, core):
        if core == 0:
            if s == 0:
                loads["wo"].wait()
                loads["wo2"].wait()
        else:
            arrived(g.at[s, :, 1 - c], FORWARD + s)
        core = c if core == 0 else 1 - c
        terms = dot_nt(g[s, :, core].reshape(256, COLS), vwo[...])
        for yy in range(NY):
            mine = terms[yy * 64:(yy + 1) * 64]
            for cb in range(4):
                for half in range(2):
                    zpart[s, yy, core, 2 * cb + half] = mine[
                        half * 32:(half + 1) * 32, cb * 128:(cb + 1) * 128
                    ]
            zpart[s, yy, core, 8] = jnp.where(low, mine[:32, 512:640], mine[32:, 512:640])

    ends = {}
    pieces = (pl.ds(0, 5), pl.ds(5, 4))

    def ring_sem(s, way, step, sub):
        return RING + ((s * 2 + way) * 4 + step) * 2 + sub

    def ring_add(s, way, step, sub, first):
        dest = (z + 4 - step) % NZ if way == 0 else (z + 4 + step) % NZ
        total = zpart[s, dest // 2, dest % 2, pieces[sub]]
        if not first:
            arrived(zr.at[s, way, step - 1, pieces[sub]], ring_sem(s, way, step - 1, sub))
            total = total + zr[s, way, step - 1, pieces[sub]].astype(F32)
        zs[s, way, step, pieces[sub]] = total.astype(BF)
        copy_to(
            zs.at[s, way, step, pieces[sub]], zr.at[s, way, step, pieces[sub]],
            at_z(1 if way == 0 else 7), ring_sem(s, way, step, sub),
        )

    def ring_start(s):
        for way in range(2):
            ring_add(s, way, 0, way, True)
        for way in range(2):
            ring_add(s, way, 1, 1 - way, True)

    def ring_step(s, step, late):
        for way in range(2):
            ring_add(s, way, step, way if late else 1 - way, False)

    def ring_end(s):
        for way in range(2):
            for sub in range(2):
                arrived(zr.at[s, way, 3, pieces[sub]], ring_sem(s, way, 3, sub))
        total = zpart[s, z // 2, z % 2] + zr[s, 0, 3].astype(F32) + zr[s, 1, 3].astype(F32)
        ends[s] = total.astype(BF)

    steps = [
        (swap_unit, 0),
        (swap_unit, 1),
        (start_unit, 0),
        (start_unit, 1),
        (swap_unit, 3),
        (swap_unit, 2),
        (start_unit, 3),
        (start_unit, 2),
        (relay_unit, 0),
        (relay_unit, 1),
        (relay_unit, 3),
        (relay_unit, 2),
        (middle_unit, 0),
        (middle_unit, 1),
        (middle_unit, 3),
        (middle_unit, 2),
        (send_queries, 0),
        (send_queries, 1),
        (attention, 0),
        (attention, 1),
        (gather_start, 0),
        (gather_start, 1),
        (gather_middle, 0),
        (gather_middle, 1),
        (gather_end, 0),
        (output_terms, 0, 0),
        (gather_end, 1),
        (output_terms, 0, 1),
        (ring_start, 0),
        (output_terms, 1, 0),
        (output_terms, 1, 1),
        (ring_start, 1),
        (ring_step, 0, 1, True),
        (ring_step, 1, 1, True),
        (ring_step, 0, 2, False),
        (ring_step, 1, 2, False),
        (ring_step, 0, 2, True),
        (ring_step, 1, 2, True),
        (ring_step, 0, 3, False),
        (ring_step, 1, 3, False),
        (ring_step, 0, 3, True),
        (ring_step, 1, 3, True),
        (ring_end, 0),
        (ring_end, 1),
    ]
    for function, *arguments in steps:
        function(*arguments)
    first, second = ends[0], ends[1]

    from_row = (k == ((r >> 1) & 1) * 64 + ((r >> 2) & 3) * 16 + (r >> 4) * 2 + (r & 1))
    to_rows = one_hot(from_row)
    for cb in range(4):
        both = jnp.concatenate(
            [first[2 * cb:2 * cb + 2].reshape(64, 128), second[2 * cb:2 * cb + 2].reshape(64, 128)], axis=0
        )
        out[:, cb * 128:(cb + 1) * 128] = dot_nn(to_rows, both).astype(BF)
    tails = jnp.concatenate([first[8], first[8], second[8], second[8]], axis=0)
    in_low = one_hot(from_row & ((k & 32) == 0))
    in_high = one_hot(from_row & ((k & 32) != 0))
    tail = dot_nn(in_low, tails) + pltpu.roll(dot_nn(in_high, tails), 64, 1)
    out[:, 512:576] = tail[:, :64].astype(BF)

    for copy in slots:
        copy.wait_send()


def local(tokens, w_query, w_keyval, w_out, cache_keys, cache_values, lengths):
    vm = pltpu.VMEM
    units = (LEFT, RIGHT, LEFT, RIGHT)
    scratch = [
        vm((2, D_LOC, 512), BF), vm((D_LOC, COLS), BF), vm((128, D_LOC), BF), vm((640, COLS), BF),
        vm((2, SLOTS, HD), BF), vm((2, SLOTS, HD), BF), pltpu.SMEM((2,), jnp.int32), vm((2, 2, 256, D_LOC), BF),
        vm((2, 256, LEFT + RIGHT), BF), vm((2, 256, LEFT + RIGHT), BF),
        *[vm((4, 4, 16, w), BF) for w in units],
        *[vm((3, 4, 16, w), BF) for w in units],
        *[vm((4, 16, w), BF) for w in units],
        *[vm((3, 16, w), BF) for w in units],
        vm((2, 128, HD), BF),
        *[vm((2, NZ, 16, HD), BF) for _ in range(4)],
        vm((2, NY, 2, NX, 16, COLS), BF),
        vm((2, NY, 2, 9, 32, 128), F32),
        vm((2, 2, 4, 9, 32, 128), BF), vm((2, 2, 4, 9, 32, 128), BF),
        pltpu.SemaphoreType.DMA((8,)), pltpu.SemaphoreType.DMA((SEND_SLOTS,)), pltpu.SemaphoreType.DMA((RELAY + 8,)),
    ]
    hbm = pl.BlockSpec(memory_space=pl.ANY)
    result = pl.pallas_call(
        kernel,
        out_shape=jax.ShapeDtypeStruct((128, D_LOC), BF),
        in_specs=[hbm] * 7,
        out_specs=pl.BlockSpec(memory_space=pltpu.VMEM),
        scratch_shapes=scratch,
        compiler_params=pltpu.CompilerParams(
            collective_id=0, has_side_effects=True, vmem_limit_bytes=56 * 2**20
        ),
        cost_estimate=pl.CostEstimate(flops=4 * 10**9, bytes_accessed=10**7, transcendentals=10**6),
        name="layer",
    )(
        tokens.transpose(1, 2, 0), w_query, w_keyval.T, w_out.T, cache_keys, cache_values, lengths
    )
    return result.reshape(64, 2, D_LOC)


def solution(mesh):
    placed = (
        P(None, None, ("batch", "gy")),
        P(("batch", "gy"), "gx"),
        P(("batch", "gy"), "gx"),
        P("gx", ("batch", "gy")),
        P(("batch", "gx", "gy"), None, None),
        P(("batch", "gx", "gy"), None, None),
        P(("batch", "gx", "gy")),
    )
    return jax.shard_map(
        local, mesh=mesh, in_specs=placed, out_specs=P("gx", None, ("batch", "gy")), check_vma=False
    )
```

```python
import functools

import jax
import jax.numpy as jnp
import numpy as np
from jax import lax
from jax.experimental import pallas as pl
from jax.experimental.pallas import tpu as pltpu
from jax.sharding import PartitionSpec as P

MESH = pl.DeviceIdType.MESH
BF = jnp.bfloat16
F32 = jnp.float32
NX, NY, NZ = 4, 4, 8
D_LOC, COLS = 576, 1536
HD, SLOTS = 256, 2048
SEND_SLOTS = 28
SWAP, STAGE1, STAGE2, QUERIES, RESULTS, GATHER1, FORWARD, GATHER2, RING, RELAY = 0, 4, 8, 12, 14, 16, 28, 30, 42, 74
RELAYED = (0, 1, 2, 3)
LEFT, RIGHT = 768, 896


def dot_nt(a, b):
    return lax.dot_general(a, b, (((1,), (1,)), ((), ())), preferred_element_type=F32)


def dot_nn(a, b):
    return lax.dot_general(a, b, (((1,), (0,)), ((), ())), preferred_element_type=F32)


def grid_of(rows, cols):
    return (
        lax.broadcasted_iota(jnp.int32, (rows, cols), 0),
        lax.broadcasted_iota(jnp.int32, (rows, cols), 1),
    )


def one_hot(hit):
    return jnp.where(hit, 1.0, 0.0).astype(BF)


def kernel(
    tok, wq, wkv, wo, ck, cv, lens_in, out,
    vtok, vwq, vwkv, vwo, vk, vv, lens, xp,
    sib_s, sib_r, part0, part1, part2, part3, got0, got1, got2, got3,
    mid0, mid1, mid2, mid3, fin0, fin1, fin2, fin3,
    stack, qs, qr, ats, atr, g, zpart, zs, zr,
    vwt, ld_sem, send_sem, recv_sem,
):
    b = lax.axis_index("batch")
    z = lax.axis_index("gx")
    x = lax.axis_index("gy")
    y, c = b // 2, b % 2

    loads = {}
    for k, (name, src, dst) in enumerate([
        ("tok", tok, vtok),
        ("wq", wq, vwq),
        ("wkv", wkv, vwkv.at[pl.ds(0, 64)]),
        ("lens", lens_in, lens),
        ("k", ck, vk),
        ("v", cv, vv),
        ("wo", wo, vwo.at[pl.ds(0, D_LOC)]),
        ("wo2", wo.at[pl.ds(512, 64)], vwo.at[pl.ds(D_LOC, 64)]),
    ]):
        loads[name] = pltpu.make_async_copy(src, dst, ld_sem.at[k])
        loads[name].start()

    def at_x(o):
        return (b, z, (x + o) % NX)

    def at_y(o):
        return ((b + 2 * o) % (2 * NY), z, x)

    def at_z(o):
        return (b, (z + o) % NZ, x)

    sibling = (y * 2 + (1 - c), z, x)

    barrier = pltpu.get_barrier_semaphore()
    partners = [sibling] + [at_x(o) for o in (1, 2, 3)] + [at_y(o) for o in (1, 2, 3)]
    partners += [at_z(o) for o in range(1, NZ)]
    for partner in partners:
        pl.semaphore_signal(barrier, inc=1, device_id=partner, device_id_type=MESH)

    slots = [None] * SEND_SLOTS
    count = [0]

    def copy_to(src, dst, device, sem):
        k = count[0] % SEND_SLOTS
        count[0] += 1
        if slots[k] is not None:
            slots[k].wait_send()
        copy = pltpu.make_async_remote_copy(
            src_ref=src, dst_ref=dst, send_sem=send_sem.at[k], recv_sem=recv_sem.at[sem],
            device_id=device, device_id_type=MESH,
        )
        copy.start()
        slots[k] = copy

    def arrived(ref, sem):
        pltpu.make_async_copy(ref, ref, recv_sem.at[sem]).wait()

    vwkv[64:128, :] = jnp.zeros((64, D_LOC), BF)
    r, k = grid_of(256, 256)
    perm = one_hot(
        k == (r & 1) * 128 + ((r >> 6) & 1) * 64 + ((r >> 1) & 7) * 8 + ((r >> 4) & 3) * 2 + (r >> 7)
    )
    loads["tok"].wait()
    for yy in range(NY):
        both = jnp.concatenate(
            [vtok[0, :, yy * 128:(yy + 1) * 128], vtok[1, :, yy * 128:(yy + 1) * 128]], axis=1
        )
        rows = dot_nt(perm, both).astype(BF)
        for s in range(2):
            for cc in range(2):
                at = (s * 2 + cc) * 64
                xp[s, cc, yy * 64:(yy + 1) * 64, :] = rows[at:at + 64]
    loads["wq"].wait()
    loads["wkv"].wait()

    first_two, last_two = pl.ds(0, 2), pl.ds(2, 2)
    parts, gots = (part0, part1, part2, part3), (got0, got1, got2, got3)
    mids, fins = (mid0, mid1, mid2, mid3), (fin0, fin1, fin2, fin3)
    first_x = (True, False, False, True)

    def project(s, side, core):
        rows = xp[s, core]
        if side == 0:
            return dot_nn(rows, vwq[:, 0:LEFT])
        return jnp.concatenate([dot_nn(rows, vwq[:, LEFT:COLS]), dot_nt(rows, vwkv[...])], axis=1)

    def width(side):
        return LEFT if side == 0 else RIGHT

    def cols_of(side):
        return pl.ds(0, LEFT) if side == 0 else pl.ds(LEFT, RIGHT)

    def swap_unit(u):
        s, side = divmod(u, 2)
        cols = cols_of(side)
        sib_s[s, :, cols] = project(s, side, 1 - c).astype(BF)
        if u == 0:
            pl.semaphore_wait(barrier, len(partners))
        copy_to(sib_s.at[s, :, cols], sib_r.at[s, :, cols], sibling, SWAP + u)

    def start_unit(u):
        s, side = divmod(u, 2)
        cols = cols_of(side)
        own = project(s, side, c)
        arrived(sib_r.at[s, :, cols], SWAP + u)
        total = (own + sib_r[s, :, cols].astype(F32)).astype(BF)
        for yy in range(NY):
            for xx in range(NX):
                at = (yy * NX + xx) * 16
                lead = (xx, yy) if first_x[u] else (yy, xx)
                parts[u][lead[0], lead[1]] = total[at:at + 16]
        me, to = (x, at_x) if first_x[u] else (y, at_y)
        if u not in RELAYED:
            for o in (2, 1, 3):
                copy_to(parts[u].at[(me + o) % 4], gots[u].at[o - 1], to(o), STAGE1 + u)
            return
        ahead, far, behind = (me + 1) % 4, (me + 2) % 4, (me + 3) % 4
        copy_to(parts[u].at[far, first_two], gots[u].at[2, first_two], to(1), RELAY + 2 * u)
        copy_to(parts[u].at[far, last_two], gots[u].at[2, last_two], to(3), RELAY + 2 * u + 1)
        copy_to(parts[u].at[ahead, last_two], gots[u].at[0, last_two], to(1), STAGE1 + u)
        copy_to(parts[u].at[behind, first_two], gots[u].at[1, first_two], to(3), STAGE1 + u)

    def relay_unit(u):
        me, to = (x, at_x) if first_x[u] else (y, at_y)
        for way, half, o in ((0, first_two, 1), (1, last_two, 3)):
            arrived(gots[u].at[2, half], RELAY + 2 * u + way)
            mine = parts[u].at[(me + o) % 4, half]
            mine[...] = (mine[...].astype(F32) + gots[u][2, half].astype(F32)).astype(BF)
            copy_to(mine, gots[u].at[way, half], to(o), STAGE1 + u)

    def middle_unit(u):
        me, to, other = (x, at_y, y) if first_x[u] else (y, at_x, x)
        came = 2 if u in RELAYED else 3
        arrived(gots[u].at[pl.ds(0, came)], STAGE1 + u)
        total = parts[u][me].astype(F32)
        for o in range(came):
            total = total + gots[u][o].astype(F32)
        mids[u][...] = total.astype(BF)
        for o in (2, 1, 3):
            copy_to(mids[u].at[(other + o) % 4], fins[u].at[o - 1], to(o), STAGE2 + u)

    def finish_unit(u):
        other = y if first_x[u] else x
        arrived(fins[u], STAGE2 + u)
        total = mids[u][other].astype(F32)
        for o in range(3):
            total = total + fins[u][o].astype(F32)
        return total.astype(BF)

    r, k = grid_of(128, 128)
    slot = r & 15
    to_groups = one_hot((slot < 14) & (k == (slot >> 1) * 16 + (r >> 4) * 2 + (slot & 1)))
    r, k = grid_of(128, 256)
    place = one_hot((r < 64) & (k == r + (z % 4) * 64))

    def send_queries(s):
        left = finish_unit(2 * s)
        right = finish_unit(2 * s + 1)
        for h in range(3):
            stack[s, h * 16:(h + 1) * 16] = left[:, h * HD:(h + 1) * HD]
            stack[s, (h + 3) * 16:(h + 4) * 16] = right[:, h * HD:(h + 1) * HD]
        stack[s, 96:112] = dot_nn(right[:, LEFT:RIGHT], place).astype(BF)
        stack[s, 112:128] = jnp.zeros((16, HD), BF)
        grouped = dot_nn(to_groups, stack[s]).astype(BF)
        for zz in range(NZ):
            qs[s, zz] = grouped[zz * 16:(zz + 1) * 16]
        for o in (4, 3, 5, 2, 6, 1, 7):
            copy_to(qs.at[s, (z + o) % NZ], qr.at[s, z], at_z(o), QUERIES + s)
        qr[s, z] = qs[s, z]

    loads["lens"].wait()
    r, k = grid_of(8, 128)
    freqs = jnp.exp(k.astype(F32) * (-np.log(10000.0) / 128))
    length = jnp.where((r & 2) == 0, lens[0], lens[1])
    angle = (length + (r & 1)).astype(F32) * freqs
    cosine, sine = jnp.cos(angle), jnp.sin(angle)

    r, k = grid_of(128, 128)
    pick_key = one_hot((r < 2) & ((k & 15) == 12 + r) & ((k >> 4) < 4))
    pick_value = one_hot((r < 2) & ((k & 15) == 12 + r) & ((k >> 4) >= 4))
    odd = (r & 1) == 1
    causal = k <= (r & 1)

    def attention(s):
        arrived(qr.at[s, pl.ds(0, NZ - 1)], QUERIES + s)
        raw = qr[s].reshape(128, HD)
        cos_rows = jnp.where(odd, cosine[2 * s + 1:2 * s + 2], cosine[2 * s:2 * s + 1])
        sin_rows = jnp.where(odd, sine[2 * s + 1:2 * s + 2], sine[2 * s:2 * s + 1])

        def rotate(values):
            u, w = values[:, :128], values[:, 128:]
            return jnp.concatenate(
                [u * cos_rows - w * sin_rows, w * cos_rows + u * sin_rows], axis=1
            ).astype(BF)

        queries = rotate(raw.astype(F32)) * (1.0 / HD**0.5)
        new_keys = rotate(dot_nn(pick_key, raw))
        new_values = dot_nn(pick_value, raw).astype(BF)
        if s == 0:
            loads["k"].wait()
        cached = dot_nt(queries, vk[s])
        _, column = grid_of(128, SLOTS)
        cached = jnp.where(column < lens[s], cached, -1e30)
        fresh = jnp.where(causal, dot_nt(queries, new_keys), -1e30)
        highest = jnp.maximum(cached.max(-1, keepdims=True), fresh.max(-1, keepdims=True))
        cached = jnp.exp(cached - highest)
        fresh = jnp.exp(fresh - highest)
        denom = cached.sum(-1, keepdims=True) + fresh.sum(-1, keepdims=True)
        if s == 0:
            loads["v"].wait()
        result = dot_nn(cached.astype(BF), vv[s]) + dot_nn(fresh.astype(BF), new_values)
        result = (result / denom).astype(BF)
        for zz in range(NZ):
            ats[s, zz] = result[zz * 16:(zz + 1) * 16]
        for o in (4, 3, 5, 2, 6, 1, 7):
            copy_to(ats.at[s, (z + o) % NZ], atr.at[s, z], at_z(o), RESULTS + s)
        atr[s, z] = ats[s, z]

    halves = (pl.ds(0, COLS // 2), pl.ds(COLS // 2, COLS // 2))
    to_heads = one_hot((r < 96) & (k == ((r >> 1) & 7) * 16 + (r >> 4) * 2 + (r & 1)))

    def gather_start(s):
        arrived(atr.at[s, pl.ds(0, NZ - 1)], RESULTS + s)
        heads = dot_nn(to_heads, atr[s].reshape(128, HD)).astype(BF)
        for h in range(6):
            g[s, y, c, x, :, h * HD:(h + 1) * HD] = heads[h * 16:(h + 1) * 16]
        mine_l = g.at[s, y, c, x, :, halves[0]]
        mine_r = g.at[s, y, c, x, :, halves[1]]
        for o in (2, 1, 3):
            copy_to(mine_l, mine_l, at_x(o), GATHER1 + s * 6 + o - 1)
            copy_to(mine_r, mine_r, at_y(o), GATHER1 + s * 6 + o + 2)
        copy_to(g.at[s, y, c, x], g.at[s, y, c, x], sibling, FORWARD + s)
        for o in (2, 1, 3):
            copy_to(mine_l, mine_l, at_y(o), GATHER2 + s * 6 + o - 1)
            copy_to(mine_r, mine_r, at_x(o), GATHER2 + s * 6 + o + 2)

    def gather_middle(s):
        for come in (1, 2, 3):
            piece_l = g.at[s, y, c, (x + 4 - come) % NX, :, halves[0]]
            piece_r = g.at[s, (y + 4 - come) % NY, c, x, :, halves[1]]
            arrived(piece_l, GATHER1 + s * 6 + come - 1)
            for o in (2, 1, 3):
                copy_to(piece_l, piece_l, at_y(o), GATHER2 + s * 6 + o - 1)
            copy_to(piece_l, piece_l, sibling, FORWARD + s)
            arrived(piece_r, GATHER1 + s * 6 + come + 2)
            for o in (2, 1, 3):
                copy_to(piece_r, piece_r, at_x(o), GATHER2 + s * 6 + o + 2)
            copy_to(piece_r, piece_r, sibling, FORWARD + s)

    def gather_end(s):
        for o in (1, 3, 2):
            block = g.at[s, (y + 4 - o) % NY, c, :, :, halves[0]]
            arrived(block, GATHER2 + s * 6 + o - 1)
            copy_to(block, block, sibling, FORWARD + s)
            block = g.at[s, :, c, (x + 4 - o) % NX, :, halves[1]]
            arrived(block, GATHER2 + s * 6 + o + 2)
            copy_to(block, block, sibling, FORWARD + s)

    low = lax.broadcasted_iota(jnp.int32, (32, 128), 1) < 64

    def prepare_output():
        loads["wo"].wait()
        loads["wo2"].wait()
        for n in range(6):
            vwt[n * 256:(n + 1) * 256] = vwo[:, n * 256:(n + 1) * 256].T

    def output_terms(s, core):
        if core == 1:
            arrived(g.at[s, :, 1 - c], FORWARD + s)
        core = c if core == 0 else 1 - c
        terms = dot_nn(g[s, :, core].reshape(256, COLS), vwt[...])
        for yy in range(NY):
            mine = terms[yy * 64:(yy + 1) * 64]
            for cb in range(4):
                for half in range(2):
                    zpart[s, yy, core, 2 * cb + half] = mine[
                        half * 32:(half + 1) * 32, cb * 128:(cb + 1) * 128
                    ]
            zpart[s, yy, core, 8] = jnp.where(low, mine[:32, 512:640], mine[32:, 512:640])

    ends = {}
    pieces = (pl.ds(0, 5), pl.ds(5, 4))

    def ring_sem(s, way, step, sub):
        return RING + ((s * 2 + way) * 4 + step) * 2 + sub

    def ring_add(s, way, step, sub, first):
        dest = (z + 4 - step) % NZ if way == 0 else (z + 4 + step) % NZ
        total = zpart[s, dest // 2, dest % 2, pieces[sub]]
        if not first:
            arrived(zr.at[s, way, step - 1, pieces[sub]], ring_sem(s, way, step - 1, sub))
            total = total + zr[s, way, step - 1, pieces[sub]].astype(F32)
        zs[s, way, step, pieces[sub]] = total.astype(BF)
        copy_to(
            zs.at[s, way, step, pieces[sub]], zr.at[s, way, step, pieces[sub]],
            at_z(1 if way == 0 else 7), ring_sem(s, way, step, sub),
        )

    def ring_start(s):
        for way in range(2):
            ring_add(s, way, 0, way, True)
        for way in range(2):
            ring_add(s, way, 1, 1 - way, True)

    def ring_step(s, step, late):
        for way in range(2):
            ring_add(s, way, step, way if late else 1 - way, False)

    def ring_end(s):
        for way in range(2):
            for sub in range(2):
                arrived(zr.at[s, way, 3, pieces[sub]], ring_sem(s, way, 3, sub))
        total = zpart[s, z // 2, z % 2] + zr[s, 0, 3].astype(F32) + zr[s, 1, 3].astype(F32)
        ends[s] = total.astype(BF)

    steps = [
        (swap_unit, 0),
        (swap_unit, 1),
        (start_unit, 0),
        (start_unit, 1),
        (swap_unit, 3),
        (swap_unit, 2),
        (start_unit, 3),
        (start_unit, 2),
        (prepare_output,),
        (relay_unit, 0),
        (relay_unit, 1),
        (relay_unit, 3),
        (relay_unit, 2),
        (middle_unit, 0),
        (middle_unit, 1),
        (middle_unit, 3),
        (middle_unit, 2),
        (send_queries, 0),
        (send_queries, 1),
        (attention, 0),
        (attention, 1),
        (gather_start, 0),
        (gather_start, 1),
        (gather_middle, 0),
        (gather_middle, 1),
        (gather_end, 0),
        (output_terms, 0, 0),
        (gather_end, 1),
        (output_terms, 0, 1),
        (ring_start, 0),
        (output_terms, 1, 0),
        (output_terms, 1, 1),
        (ring_start, 1),
        (ring_step, 0, 1, True),
        (ring_step, 1, 1, True),
        (ring_step, 0, 2, False),
        (ring_step, 1, 2, False),
        (ring_step, 0, 2, True),
        (ring_step, 1, 2, True),
        (ring_step, 0, 3, False),
        (ring_step, 1, 3, False),
        (ring_step, 0, 3, True),
        (ring_step, 1, 3, True),
        (ring_end, 0),
        (ring_end, 1),
    ]
    for function, *arguments in steps:
        function(*arguments)
    first, second = ends[0], ends[1]

    from_row = (k == ((r >> 1) & 1) * 64 + ((r >> 2) & 3) * 16 + (r >> 4) * 2 + (r & 1))
    to_rows = one_hot(from_row)
    for cb in range(4):
        both = jnp.concatenate(
            [first[2 * cb:2 * cb + 2].reshape(64, 128), second[2 * cb:2 * cb + 2].reshape(64, 128)], axis=0
        )
        out[:, cb * 128:(cb + 1) * 128] = dot_nn(to_rows, both).astype(BF)
    tails = jnp.concatenate([first[8], first[8], second[8], second[8]], axis=0)
    in_low = one_hot(from_row & ((k & 32) == 0))
    in_high = one_hot(from_row & ((k & 32) != 0))
    tail = dot_nn(in_low, tails) + pltpu.roll(dot_nn(in_high, tails), 64, 1)
    out[:, 512:576] = tail[:, :64].astype(BF)

    for copy in slots:
        copy.wait_send()


def local(tokens, w_query, w_keyval, w_out, cache_keys, cache_values, lengths):
    vm = pltpu.VMEM
    units = (LEFT, RIGHT, LEFT, RIGHT)
    scratch = [
        vm((2, D_LOC, 512), BF), vm((D_LOC, COLS), BF), vm((128, D_LOC), BF), vm((640, COLS), BF),
        vm((2, SLOTS, HD), BF), vm((2, SLOTS, HD), BF), pltpu.SMEM((2,), jnp.int32), vm((2, 2, 256, D_LOC), BF),
        vm((2, 256, LEFT + RIGHT), BF), vm((2, 256, LEFT + RIGHT), BF),
        *[vm((4, 4, 16, w), BF) for w in units],
        *[vm((3, 4, 16, w), BF) for w in units],
        *[vm((4, 16, w), BF) for w in units],
        *[vm((3, 16, w), BF) for w in units],
        vm((2, 128, HD), BF),
        *[vm((2, NZ, 16, HD), BF) for _ in range(4)],
        vm((2, NY, 2, NX, 16, COLS), BF),
        vm((2, NY, 2, 9, 32, 128), F32),
        vm((2, 2, 4, 9, 32, 128), BF), vm((2, 2, 4, 9, 32, 128), BF),
        vm((COLS, 640), BF),
        pltpu.SemaphoreType.DMA((8,)), pltpu.SemaphoreType.DMA((SEND_SLOTS,)), pltpu.SemaphoreType.DMA((RELAY + 8,)),
    ]
    hbm = pl.BlockSpec(memory_space=pl.ANY)
    result = pl.pallas_call(
        kernel,
        out_shape=jax.ShapeDtypeStruct((128, D_LOC), BF),
        in_specs=[hbm] * 7,
        out_specs=pl.BlockSpec(memory_space=pltpu.VMEM),
        scratch_shapes=scratch,
        compiler_params=pltpu.CompilerParams(
            collective_id=0, has_side_effects=True, vmem_limit_bytes=56 * 2**20
        ),
        cost_estimate=pl.CostEstimate(flops=4 * 10**9, bytes_accessed=10**7, transcendentals=10**6),
        name="layer",
    )(
        tokens.transpose(1, 2, 0), w_query, w_keyval.T, w_out.T, cache_keys, cache_values, lengths
    )
    return result.reshape(64, 2, D_LOC)


def solution(mesh):
    placed = (
        P(None, None, ("batch", "gy")),
        P(("batch", "gy"), "gx"),
        P(("batch", "gy"), "gx"),
        P("gx", ("batch", "gy")),
        P(("batch", "gx", "gy"), None, None),
        P(("batch", "gx", "gy"), None, None),
        P(("batch", "gx", "gy")),
    )
    return jax.shard_map(
        local, mesh=mesh, in_specs=placed, out_specs=P("gx", None, ("batch", "gy")), check_vma=False
    )
```
